256 devices in a mesh: outer: 8 (over z_hi, core), inner: 32 (over y, x, z_lo).
Axes of the slice: x: 4, y: 4, z: 8 (z_hi: 4, z_lo: 2; z = z_hi * 2 + z_lo), core: 2. Of those that a mesh axis runs over, the one named last changes fastest.
Arguments:
- object_field: float32 [2, 2048, 8192], P(None, ('outer', 'inner')), may hold values from -6 to 6
- probe: float32 [2, 2048, 8192], P(None, ('outer', 'inner')), may hold values from -8 to 8
- intensity: float32 [2048, 8192], P(('outer', 'inner')), may hold values from 0.01 to 9
- row_offset: int32 [1], replicated, may hold values from 1 to 7
- col_offset: int32 [1], replicated, may hold values from 0 to 8191
Outputs:
- object_step: float32 [2, 2048, 8192], P(None, ('outer', 'inner'))
The draws below stay inside these ranges and needn't reach their ends.
All inputs are finite; a program needn't handle non-finite values.
Results may differ from the reference program's by a relative error of at most 0.00013.
Values sent between devices are 32-bit elements; how exact they have to be, the bound alone decides.
A program may use at most 128 MiB of HBM per device.

```python
import math
import jax
import jax.numpy as jnp
from jax import lax

NCOL = 8192
ROWS_DEV = 8
NROW = 2048
N_OUTER = 8


def draw_probe(key, part):
    key = jax.random.fold_in(key, 11)
    row_level = jnp.arange(NROW, dtype=jnp.float32) / NROW
    envelope = jnp.exp(jnp.log(3.0) * row_level)
    base = 0.5 * jnp.clip(jax.random.normal(key, (2, NROW, NCOL), jnp.float32), -5.0, 5.0)
    return (base * envelope[None, :, None]).astype(jnp.float32)


def level_of(key, dims, cuts, smallest, high):
    gain, own = 1.0, jax.random.fold_in(key, 6)
    for axis_at, blocks in cuts:
        steps = jnp.exp(jax.random.uniform(jax.random.fold_in(own, axis_at), (blocks,), jnp.float32, smallest / len(cuts), high / len(cuts)))
        gain = gain * jnp.repeat(steps, dims[axis_at] // blocks).reshape([-1 if axis == axis_at else 1 for axis in range(len(dims))])
    return gain


def centred(key, shape, spread, limit, cuts=(), kind=jnp.bfloat16):
    gain = level_of(key, shape, cuts, -0.22, 0.18) if cuts else 1.0
    drawn = jax.random.normal(key, shape, jnp.float32) * spread * gain
    return jnp.minimum(jnp.maximum(drawn, -limit), limit).astype(kind)


def setup_inputs(seed: int = 0) -> dict:
    key_list = jax.random.split(jax.random.key(seed), 6)
    return {
        "object_field": centred(key_list[0], (2, NROW, NCOL), 1.0, 6.0, ((1, 256),), jnp.float32),
        "probe": draw_probe(jax.random.fold_in(key_list[5], 71), 0),
        "intensity": jnp.clip(jnp.exp(math.log(9.0) - 6.802395 * jax.random.uniform(key_list[2], (NROW, NCOL), jnp.float32) ** level_of(key_list[2], (NROW, NCOL), ((0, 256),), -0.2, 0.2)), 0.01, 9.0),
        "row_offset": jax.random.randint(key_list[3], (1,), 1, ROWS_DEV).astype(jnp.int32),
        "col_offset": jax.random.randint(key_list[4], (1,), 0, NCOL).astype(jnp.int32),
    }


FLOOR_LEVEL = 0.1

def bit_reverse(values, bit_count):
    result = jnp.zeros_like(values)
    for position in range(bit_count):
        result = result + values // (1 << position) % 2 * (1 << bit_count - 1 - position)
    return result

def reference(object_field, probe, intensity, row_offset, col_offset):
    view = jnp.roll(object_field, (row_offset[0], col_offset[0]), axis=(1, 2))
    row_index = jnp.arange(NROW, dtype=jnp.int32) - NROW // 2
    col_index = jnp.arange(NCOL, dtype=jnp.int32) - NCOL // 2
    row_phase = math.pi / NROW * (row_index * row_index % (2 * NROW)).astype(jnp.float32)
    col_phase = math.pi / NCOL * (col_index * col_index % (2 * NCOL)).astype(jnp.float32)
    phase = row_phase[:, None] + col_phase[None, :]
    chirp = lax.complex(jnp.cos(phase), jnp.sin(phase))
    probe_wave = lax.complex(probe[0], probe[1])
    view_wave = lax.complex(view[0], view[1])
    exit_wave = probe_wave * view_wave
    spectrum = jnp.fft.fft2(exit_wave * chirp, norm='ortho')
    freq_rows = jnp.arange(NROW, dtype=jnp.int32)
    bit_count = N_OUTER.bit_length() - 1
    source_rows = NROW // N_OUTER * bit_reverse(freq_rows % N_OUTER, bit_count) + freq_rows // N_OUTER
    detector = intensity[source_rows]
    magnitude = jnp.abs(spectrum)
    replaced = spectrum * (jnp.sqrt(detector) / jnp.maximum(magnitude, FLOOR_LEVEL))
    revised = jnp.fft.ifft2(replaced, norm='ortho') * jnp.conj(chirp)
    peak = jnp.max(probe[0] * probe[0] + probe[1] * probe[1])
    step_wave = jnp.conj(probe_wave) * (revised - exit_wave) / peak
    return jnp.stack([jnp.real(step_wave), jnp.imag(step_wave)]).astype(jnp.float32)
```

```python
import math

import jax
import jax.numpy as jnp
import numpy as np
from jax import lax
from jax.experimental import pallas as pl
from jax.experimental.pallas import tpu as pltpu
from jax.sharding import PartitionSpec as P

FLOOR_LEVEL = 0.1
MESH = pl.DeviceIdType.MESH
CHIPS = 128
F32 = jnp.float32
BF16 = jnp.bfloat16


def split_table(table):
    table = np.asarray(table, np.float64).astype(np.float32)
    high = table.astype(jnp.bfloat16)
    low = (table - high.astype(np.float32)).astype(jnp.bfloat16)
    return np.stack([high, low])


def turn(numerator, modulus):
    angle = -2.0 * np.pi * (np.asarray(numerator) % modulus) / modulus
    return np.exp(1j * angle)


def expanded(table):
    return np.block([[table.real, table.imag], [-table.imag, table.real]])


def make_tables():
    tables = {}
    col = np.arange(8192, dtype=np.int64) - 4096
    col_phase = np.pi / 8192 * (col * col % 16384)
    tables["col_chirp"] = np.stack([np.cos(col_phase), np.sin(col_phase)]).reshape(2, 1, 8192).astype(np.float32)
    row = np.arange(2048, dtype=np.int64) - 1024
    row_phase = (np.pi / 2048 * (row * row % 4096)).reshape(256, 8).T
    tables["row_chirp"] = np.stack([np.cos(row_phase), np.sin(row_phase)]).astype(np.float32)
    order = np.concatenate([2 * np.arange(64), 2 * np.arange(64) + 1])
    first = turn(np.arange(128)[:, None] * order[None, :], 128)
    tables["first"] = split_table(np.concatenate([first.real, first.imag], axis=1))
    back = np.conj(first).T
    tables["first_back"] = split_table(np.concatenate([back.real, back.imag], axis=1))
    chip_turn = turn(np.arange(64)[:, None] * np.arange(128)[None, :], 8192)
    tables["chip_turn"] = np.stack([chip_turn.real, chip_turn.imag]).astype(np.float32)
    base = []
    for core in range(2):
        blocks = []
        for zh in range(4):
            halves = []
            for half in range(2):
                q = 32 * (core if half == 0 else 1 - core) + np.arange(32)
                klow = np.arange(4)
                m = np.arange(64)
                power = (
                    m[:, None, None] * q[None, None, :] * 8
                    + zh * klow[None, :, None] * 128
                    + core * klow[None, :, None] * 64
                )
                halves.append(expanded(turn(power, 512).reshape(64, 128)))
            blocks.append(np.concatenate(halves, axis=1))
        base.append(np.concatenate(blocks, axis=0))
    tables["base"] = np.stack(base).astype(np.float32)
    index = np.arange(256)
    zl, y, x, l = index // 128, index // 32 % 4, index // 8 % 4, index % 8
    n = 64 * y + 16 * x + 8 * zl + l
    last = turn(n[:, None] * n[None, :], 256)
    tables["last"] = split_table(np.block([[last.real, -last.imag], [last.imag, last.real]]))
    tables["last_back"] = split_table(np.block([[last.real, last.imag], [-last.imag, last.real]]))
    klow = np.arange(128) // 32
    twiddle = np.stack([turn(n[:, None] * (klow[None, :] + 4 * k2), 2048) for k2 in range(2)]) / 4096.0
    tables["twiddle"] = np.stack([twiddle.real, twiddle.imag], axis=1).astype(np.float32)
    return tables


TABLES = (
    "col_chirp",
    "row_chirp",
    "first",
    "first_back",
    "chip_turn",
    "base",
    "last",
    "last_back",
    "twiddle",
)


def split(value):
    high = value.astype(BF16)
    low = (value - high.astype(F32)).astype(BF16)
    return high, low


def dot(left, right):
    return jnp.dot(left, right, preferred_element_type=F32)


def dot_t(left, right):
    return lax.dot_general(left, right, (((1,), (1,)), ((), ())), preferred_element_type=F32)


def three(op, left, right):
    return op(left[0], right[0]) + (op(left[0], right[1]) + op(left[1], right[0]))


def device_of(chip, core):
    z = chip // 16
    return (z // 2) * 2 + core, (chip // 4 % 4) * 8 + (chip % 4) * 2 + z % 2


def flip(chip, offset):
    return chip ^ offset


def tile(ref, index):
    return ref.at[pl.ds(pl.multiple_of(index * 8, 8), 8)]


def kernel(
    row_off,
    col_off,
    obj_hbm,
    probe_hbm,
    int_hbm,
    col_chirp_hbm,
    row_chirp_hbm,
    first_hbm,
    first_back_hbm,
    chip_turn_hbm,
    base_hbm,
    last_hbm,
    last_back_hbm,
    twiddle_hbm,
    out_ref,
    peak_ref,
    obj,
    probe,
    inten,
    col_chirp,
    row_chirp,
    first,
    first_back,
    chip_turn,
    base,
    last,
    last_back,
    twiddle,
    rolled,
    arrived,
    wave,
    turned,
    field_out,
    field_in,
    mixed,
    mixed_out,
    factor,
    spread,
    shades_out,
    shades_in,
    back_out,
    back_in,
    part_out,
    part_in,
    peak_own,
    peak_z,
    peak_y,
    peak_x,
    peak_c,
    load_sem,
    shift_sem,
    int_sem,
    z_sem,
    y_sem,
    x_sem,
    c_sem,
    shade_sem,
    pass_sem,
    field_sem,
    mix_sem,
    part_sem,
    back_sem,
    local_sem,
):
    outer, inner = lax.axis_index("outer"), lax.axis_index("inner")
    zh, core = outer // 2, outer % 2
    other = 1 - core
    chip = (zh * 2 + inner % 2) * 16 + (inner // 8) * 4 + inner // 2 % 4
    number = outer * 32 + inner
    after, before = (number + 1) % 256, (number + 255) % 256
    sibling = device_of(chip, other)
    next_device = (after // 32, after % 32)
    last_device = (before // 32, before % 32)

    loads = []
    pairs = (
        (obj_hbm, obj),
        (probe_hbm, probe),
        (int_hbm, inten.at[core]),
        (base_hbm.at[core], base),
        (chip_turn_hbm, chip_turn),
        (col_chirp_hbm, col_chirp),
        (row_chirp_hbm, row_chirp),
        (first_hbm, first),
        (last_hbm, last),
        (last_back_hbm, last_back),
        (twiddle_hbm, twiddle),
        (first_back_hbm, first_back),
    )
    for slot, (source, target) in enumerate(pairs):
        copy = pltpu.make_async_copy(source, target, load_sem.at[slot])
        copy.start()
        loads.append(copy)

    barrier = pltpu.get_barrier_semaphore()
    greeted = [device_of(flip(chip, k << 4), core) for k in range(1, 8)]
    greeted += [device_of(flip(chip, k << 2), core) for k in range(1, 4)]
    greeted += [device_of(flip(chip, k), core) for k in range(1, 4)]
    greeted += [sibling, next_device, last_device]
    for device in greeted:
        pl.semaphore_signal(barrier, inc=1, device_id=device, device_id_type=MESH)

    rows_by, cols_by = row_off[0], col_off[0]
    tiles_by, lanes_by = cols_by // 128, cols_by % 128
    lane = lax.broadcasted_iota(jnp.int32, (8, 128), 1)
    sub = lax.broadcasted_iota(jnp.int32, (8, 128), 0)
    loads[0].wait()
    for part in range(2):

        def roll_step(step, carry, part=part):
            for inside in range(8):
                at = step * 8 + inside
                piece = obj[part, :, pl.ds(pl.multiple_of(at * 128, 128), 128)]
                moved = pltpu.roll(pltpu.roll(piece, lanes_by, 1), rows_by, 0)
                rolled[pl.ds(part * 64 + at, 8, stride=128), :] = moved
            return carry

        lax.fori_loop(0, 8, roll_step, 0)
    wide_lane = lax.broadcasted_iota(jnp.int32, (64, 128), 1)

    def tile_step(block, carry):
        at = pl.ds(pl.multiple_of(block * 64, 64), 64)
        moved = pltpu.roll(rolled[at, :], tiles_by, 0)
        rolled[at, :] = jnp.where(wide_lane < lanes_by, pltpu.roll(moved, 1, 0), moved)
        return carry

    lax.fori_loop(0, 16, tile_step, 0)
    arrived[pl.ds(896, 128), :] = jnp.zeros((128, 128), F32)

    pl.semaphore_wait(barrier, 16)

    shift = pltpu.make_async_remote_copy(
        src_ref=rolled.at[pl.ds(0, 896)],
        dst_ref=arrived.at[pl.ds(0, 896)],
        send_sem=shift_sem.at[0],
        recv_sem=shift_sem.at[1],
        device_id=next_device,
        device_id_type=MESH,
    )
    shift.start()
    loads[2].wait()
    share = pltpu.make_async_remote_copy(
        src_ref=inten.at[core],
        dst_ref=inten.at[core],
        send_sem=int_sem.at[0],
        recv_sem=int_sem.at[1],
        device_id=sibling,
        device_id_type=MESH,
    )
    share.start()

    loads[1].wait()

    def peak_step(step, best):
        for inside in range(8):
            at = pl.ds(pl.multiple_of((step * 8 + inside) * 128, 128), 128)
            real, imag = probe[0, :, at], probe[1, :, at]
            best = jnp.maximum(best, real * real + imag * imag)
        return best

    peak_own[0] = lax.fori_loop(0, 8, peak_step, jnp.zeros((8, 128), F32))

    def peak_line(source, target, sem, count, by):
        copies = []
        for k in range(1, count):
            copy = pltpu.make_async_remote_copy(
                src_ref=source,
                dst_ref=target.at[k - 1],
                send_sem=sem.at[k - 1],
                recv_sem=sem.at[count - 2 + k],
                device_id=device_of(flip(chip, k << by), core),
                device_id_type=MESH,
            )
            copy.start()
            copies.append(copy)
        return copies

    z_line = peak_line(peak_own.at[0], peak_z, z_sem, 8, 4)

    loads[3].wait()
    loads[4].wait()
    chip_lane = lax.broadcasted_iota(jnp.int32, (64, 128), 1) == chip
    turn_re = jnp.sum(jnp.where(chip_lane, chip_turn[0], 0.0), axis=1, keepdims=True)
    turn_im = jnp.sum(jnp.where(chip_lane, chip_turn[1], 0.0), axis=1, keepdims=True)
    for block in range(4):
        low, high = pl.ds(block * 128, 64), pl.ds(block * 128 + 64, 64)
        for_re, for_im = base[low, :], base[high, :]
        for at, value in (
            (low, for_re * turn_re + for_im * turn_im),
            (high, for_im * turn_re - for_re * turn_im),
        ):
            high_part, low_part = split(value)
            mixed[0, at, :] = high_part
            mixed[1, at, :] = low_part

    for copy in z_line:
        copy.wait_recv()
    best = peak_own[0]
    for k in range(7):
        best = jnp.maximum(best, peak_z[k])
    peak_own[1] = best
    y_line = peak_line(peak_own.at[1], peak_y, y_sem, 4, 2)

    share.wait_recv()
    for c in range(2):

        def spread_step(step, carry, c=c):
            for inside in range(8):
                at = step * 8 + inside
                piece = inten[c, :, pl.ds(pl.multiple_of(at * 128, 128), 128)]
                spread[pl.ds(c * 64 + at, 8, stride=128), :] = piece
            return carry

        lax.fori_loop(0, 8, spread_step, 0)
    for l in range(4):
        shades_out[pl.ds(l, 128, stride=8), :] = jnp.transpose(spread[pl.ds(l * 128, 128), :])

    for copy in y_line:
        copy.wait_recv()
    for k in range(3):
        best = jnp.maximum(best, peak_y[k])
    peak_own[2] = best
    x_line = peak_line(peak_own.at[2], peak_x, x_sem, 4, 0)
    for l in range(4, 8):
        shades_out[pl.ds(l, 128, stride=8), :] = jnp.transpose(spread[pl.ds(l * 128, 128), :])
    for copy in x_line:
        copy.wait_recv()
    for k in range(3):
        best = jnp.maximum(best, peak_x[k])
    peak_own[3] = best
    c_line = pltpu.make_async_remote_copy(
        src_ref=peak_own.at[3],
        dst_ref=peak_c,
        send_sem=c_sem.at[0],
        recv_sem=c_sem.at[1],
        device_id=sibling,
        device_id_type=MESH,
    )
    c_line.start()

    def shade_step(step, carry):
        target = flip(chip, 2 * step + core)
        pltpu.make_async_remote_copy(
            src_ref=tile(shades_out, target),
            dst_ref=shades_in.at[chip // 2, chip % 2],
            send_sem=shade_sem.at[0],
            recv_sem=shade_sem.at[1],
            device_id=device_of(target, core),
            device_id_type=MESH,
        ).start()
        return carry

    lax.fori_loop(1, 64, shade_step, 0)

    @pl.when(core == 1)
    def _():
        shade_step(0, 0)

    @pl.when(core == 0)
    def _():
        own = pltpu.make_async_copy(
            tile(shades_out, chip), shades_in.at[chip // 2, chip % 2], local_sem.at[0]
        )
        own.start()
        own.wait()

    for slot in (5, 6, 7):
        loads[slot].wait()
    number_lane = lax.broadcasted_iota(jnp.int32, (8, 256), 1) == number
    row_re = jnp.sum(jnp.where(number_lane, row_chirp[0], 0.0), axis=1, keepdims=True)
    row_im = jnp.sum(jnp.where(number_lane, row_chirp[1], 0.0), axis=1, keepdims=True)

    def chirp_at(at):
        col_re, col_im = col_chirp[0, :, at], col_chirp[1, :, at]
        return row_re * col_re - row_im * col_im, row_re * col_im + row_im * col_re

    shift.wait_recv()

    def wave_step(step, carry):
        for inside in range(8):
            index = step * 8 + inside
            at = pl.ds(pl.multiple_of(index * 128, 128), 128)
            views = []
            for part in range(2):
                rows = pl.ds(part * 64 + index, 8, stride=128)
                views.append(jnp.where(sub < rows_by, arrived[rows, :], rolled[rows, :]))
            probe_re, probe_im = probe[0, :, at], probe[1, :, at]
            real = probe_re * views[0] - probe_im * views[1]
            imag = probe_re * views[1] + probe_im * views[0]
            wave[0, :, at] = real
            wave[1, :, at] = imag
            chirp_re, chirp_im = chirp_at(at)
            real, imag = real * chirp_re - imag * chirp_im, real * chirp_im + imag * chirp_re
            even = jnp.where(lane < 64, real, pltpu.roll(imag, 64, 1))
            odd = jnp.where(lane < 64, pltpu.roll(real, 64, 1), imag)
            turned[pl.ds(index, 8, stride=128), :] = even
            turned[pl.ds(64 + index, 8, stride=128), :] = odd
        return carry

    lax.fori_loop(0, 8, wave_step, 0)

    def times_i(value):
        half = lax.broadcasted_iota(jnp.int32, value.shape, 1) < 64
        moved = pltpu.roll(value, 64, 1)
        return jnp.where(half, -moved, moved)

    def first_step(load, table, store):
        for pair in range(4):
            sides = []
            for row in (2 * pair, 2 * pair + 1):
                value = load(row)
                sides.append(jnp.concatenate([value, times_i(value)], axis=0))
            result = three(dot, (table[0], table[1]), split(jnp.concatenate(sides, axis=1)))
            store(2 * pair, result[:, :128])
            store(2 * pair + 1, result[:, 128:])

    def store_field(row, value):
        field_out[pl.ds(row, 128, stride=8), :] = value

    first_step(lambda row: turned[pl.ds(row * 128, 128), :], first, store_field)

    def send_all(source, target, sem):
        def send_step(k, carry):
            to = flip(chip, k)
            pltpu.make_async_remote_copy(
                src_ref=tile(source, to),
                dst_ref=tile(target, chip),
                send_sem=sem.at[0],
                recv_sem=sem.at[1],
                device_id=device_of(to, core),
                device_id_type=MESH,
            ).start()
            return carry

        lax.fori_loop(1, 128, send_step, 0)
        own = pltpu.make_async_copy(tile(source, chip), tile(target, chip), local_sem.at[0])
        own.start()
        own.wait()

    def all_of(source, target, sem, rows):
        return pltpu.make_async_remote_copy(
            src_ref=source.at[pl.ds(0, rows)],
            dst_ref=target.at[pl.ds(0, rows)],
            send_sem=sem.at[0],
            recv_sem=sem.at[1],
            device_id=sibling,
            device_id_type=MESH,
        )

    send_all(field_out, field_in, field_sem)

    @pl.when(core == 0)
    def _():
        all_of(shades_out, field_in, shade_sem, 504).wait()

    @pl.when(core == 1)
    def _():
        all_of(shades_out, field_in, shade_sem, 512).wait()

    mine = (chip + core) % 2
    hand_over = pltpu.make_async_remote_copy(
        src_ref=shades_in.at[:, mine],
        dst_ref=shades_in.at[:, mine],
        send_sem=pass_sem.at[0],
        recv_sem=pass_sem.at[1],
        device_id=sibling,
        device_id_type=MESH,
    )
    hand_over.start()
    hand_over.wait()
    group = lax.broadcasted_iota(jnp.int32, (256, 128), 1) // 32
    for c in range(2):
        shade = jnp.zeros((256, 128), F32)
        for digit in range(4):
            want = 2 * (digit % 2) + digit // 2
            by = (32 * (want - 2 * c - core) + 128) % 128
            part = shades_in[pl.ds(digit * 16, 16)].reshape(256, 128)
            shade = jnp.where(group == want, pltpu.roll(part, by, 1), shade)
        factor[c] = jnp.sqrt(shade)
    c_line.wait_recv()
    peak_ref[...] = jnp.maximum(best, peak_c[...])

    all_of(field_out, field_in, field_sem, 1016).wait()
    joined = jnp.concatenate([field_in[pl.ds(digit * 256, 256), :] for digit in range(4)], axis=1)
    joined = split(joined)
    mixed_table = (mixed[0], mixed[1])
    result = three(dot, joined, mixed_table)
    mixed_out[0] = result[:, 256:]
    mix = pltpu.make_async_remote_copy(
        src_ref=mixed_out.at[0],
        dst_ref=mixed_out.at[1],
        send_sem=mix_sem.at[0],
        recv_sem=mix_sem.at[1],
        device_id=sibling,
        device_id_type=MESH,
    )
    mix.start()
    kept = result[:, :256]
    loads[8].wait()
    loads[10].wait()
    mix.wait_recv()
    got = mixed_out[1]
    sign = jnp.where(core == 0, 1.0, -1.0).astype(F32)
    sums = (kept + got, (kept - got) * sign)
    data = []
    for k2 in range(2):
        real, imag = sums[k2][:, :128], sums[k2][:, 128:]
        turn_r, turn_i = twiddle[k2, 0], twiddle[k2, 1]
        data.append(
            jnp.concatenate([real * turn_r - imag * turn_i, real * turn_i + imag * turn_r], axis=0)
        )
    spectrum = three(dot, (last[0], last[1]), split(jnp.concatenate(data, axis=1)))
    data = []
    for k2 in range(2):
        real = spectrum[:256, k2 * 128 : (k2 + 1) * 128]
        imag = spectrum[256:, k2 * 128 : (k2 + 1) * 128]
        scale = factor[k2] / jnp.maximum(jnp.sqrt(real * real + imag * imag), FLOOR_LEVEL)
        data.append(jnp.concatenate([real * scale, imag * scale], axis=0))
    loads[9].wait()
    field = three(dot, (last_back[0], last_back[1]), split(jnp.concatenate(data, axis=1)))
    parts = []
    for k2 in range(2):
        real = field[:256, k2 * 128 : (k2 + 1) * 128]
        imag = field[256:, k2 * 128 : (k2 + 1) * 128]
        turn_r, turn_i = twiddle[k2, 0], twiddle[k2, 1]
        parts.append(
            jnp.concatenate([real * turn_r + imag * turn_i, imag * turn_r - real * turn_i], axis=1)
        )
    plus, minus = parts[0] + parts[1], parts[0] - parts[1]
    own_core = core == 0
    part_out[...] = jnp.where(own_core, minus, plus)
    swap = pltpu.make_async_remote_copy(
        src_ref=part_out,
        dst_ref=part_in,
        send_sem=part_sem.at[0],
        recv_sem=part_sem.at[1],
        device_id=sibling,
        device_id_type=MESH,
    )
    swap.start()
    own = jnp.where(own_core, plus, minus)
    swap.wait_recv()
    joined = split(jnp.concatenate([own, part_in[...]], axis=1))
    result = three(dot_t, joined, mixed_table)
    for digit in range(4):
        back_out[pl.ds(digit * 256, 256), :] = result[:, digit * 128 : (digit + 1) * 128]
    send_all(back_out, back_in, back_sem)

    loads[11].wait()
    all_of(back_out, back_in, back_sem, 1016).wait()

    def store_turned(row, value):
        turned[pl.ds(row * 128, 128), :] = value

    first_step(lambda row: back_in[pl.ds(row, 128, stride=8), :], first_back, store_turned)

    def last_step(step, carry):
        for inside in range(8):
            index = step * 8 + inside
            at = pl.ds(pl.multiple_of(index * 128, 128), 128)
            even = turned[pl.ds(index, 8, stride=128), :]
            odd = turned[pl.ds(64 + index, 8, stride=128), :]
            real = jnp.where(lane < 64, even, pltpu.roll(odd, 64, 1))
            imag = jnp.where(lane < 64, pltpu.roll(even, 64, 1), odd)
            chirp_re, chirp_im = chirp_at(at)
            step_re = real * chirp_re + imag * chirp_im - wave[0, :, at]
            step_im = imag * chirp_re - real * chirp_im - wave[1, :, at]
            probe_re, probe_im = probe[0, :, at], probe[1, :, at]
            out_ref[0, :, at] = probe_re * step_re + probe_im * step_im
            out_ref[1, :, at] = probe_re * step_im - probe_im * step_re
        return carry

    lax.fori_loop(0, 8, last_step, 0)

    shift.wait_send()
    share.wait_send()
    for copy in z_line + y_line + x_line:
        copy.wait_send()
    c_line.wait_send()
    mix.wait_send()
    swap.wait_send()


def body(object_field, probe, intensity, row_offset, col_offset):
    tables = make_tables()
    constants = [jnp.asarray(tables[name]) for name in TABLES]
    vmem, dma = pltpu.VMEM, pltpu.SemaphoreType.DMA
    anywhere = pl.BlockSpec(memory_space=pl.ANY)
    scalar = pl.BlockSpec(memory_space=pltpu.SMEM)
    inside = pl.BlockSpec(memory_space=pltpu.VMEM)
    state = vmem((1024, 128), F32)
    scratch = [
        vmem((2, 8, 8192), F32),
        vmem((2, 8, 8192), F32),
        vmem((2, 8, 8192), F32),
        vmem((2, 1, 8192), F32),
        vmem((2, 8, 256), F32),
        vmem((2, 128, 256), BF16),
        vmem((2, 128, 256), BF16),
        vmem((2, 64, 128), F32),
        vmem((512, 512), F32),
        vmem((2, 512, 512), BF16),
        vmem((2, 512, 512), BF16),
        vmem((2, 2, 256, 128), F32),
        state,
        state,
        vmem((2, 8, 8192), F32),
        state,
        state,
        state,
        vmem((2, 512, 512), BF16),
        vmem((2, 256, 256), F32),
        vmem((2, 256, 128), F32),
        state,
        state,
        vmem((64, 2, 8, 128), F32),
        state,
        state,
        vmem((256, 256), F32),
        vmem((256, 256), F32),
        vmem((4, 8, 128), F32),
        vmem((7, 8, 128), F32),
        vmem((3, 8, 128), F32),
        vmem((3, 8, 128), F32),
        vmem((8, 128), F32),
        dma((12,)),
        dma((2,)),
        dma((2,)),
        dma((14,)),
        dma((6,)),
        dma((6,)),
        dma((2,)),
        dma((2,)),
        dma((2,)),
        dma((2,)),
        dma((2,)),
        dma((2,)),
        dma((2,)),
        dma((1,)),
    ]
    step, peak = pl.pallas_call(
        kernel,
        out_shape=(
            jax.ShapeDtypeStruct(object_field.shape, F32),
            jax.ShapeDtypeStruct((8, 128), F32),
        ),
        in_specs=[scalar, scalar] + [anywhere] * (3 + len(constants)),
        out_specs=(inside, inside),
        scratch_shapes=scratch,
        compiler_params=pltpu.CompilerParams(
            collective_id=0, has_side_effects=True, vmem_limit_bytes=40 << 20
        ),
        cost_estimate=pl.CostEstimate(
            flops=2_000_000_000, bytes_accessed=8_000_000, transcendentals=200_000
        ),
    )(row_offset, col_offset, object_field, probe, intensity, *constants)
    return step / jnp.max(peak)


def solution(mesh):
    placed = (
        P(None, ("outer", "inner"), None),
        P(None, ("outer", "inner"), None),
        P(("outer", "inner"), None),
        P(),
        P(),
    )
    return jax.shard_map(
        body,
        mesh=mesh,
        in_specs=placed,
        out_specs=P(None, ("outer", "inner"), None),
        check_vma=False,
    )
```

```python
import math

import jax
import jax.numpy as jnp
import numpy as np
from jax import lax
from jax.experimental import pallas as pl
from jax.experimental.pallas import tpu as pltpu
from jax.sharding import PartitionSpec as P

FLOOR_LEVEL = 0.1
EARLY = 3
MESH = pl.DeviceIdType.MESH
CHIPS = 128
F32 = jnp.float32
BF16 = jnp.bfloat16


def split_table(table):
    table = np.asarray(table, np.float64).astype(np.float32)
    high = table.astype(jnp.bfloat16)
    low = (table - high.astype(np.float32)).astype(jnp.bfloat16)
    return np.stack([high, low])


def turn(numerator, modulus):
    angle = -2.0 * np.pi * (np.asarray(numerator) % modulus) / modulus
    return np.exp(1j * angle)


def expanded(table):
    return np.block([[table.real, table.imag], [-table.imag, table.real]])


def make_tables():
    tables = {}
    col = np.arange(8192, dtype=np.int64) - 4096
    col_phase = np.pi / 8192 * (col * col % 16384)
    tables["col_chirp"] = np.stack([np.cos(col_phase), np.sin(col_phase)]).reshape(2, 1, 8192).astype(np.float32)
    row = np.arange(2048, dtype=np.int64) - 1024
    row_phase = (np.pi / 2048 * (row * row % 4096)).reshape(256, 8).T
    tables["row_chirp"] = np.stack([np.cos(row_phase), np.sin(row_phase)]).astype(np.float32)
    order = np.concatenate([2 * np.arange(64), 2 * np.arange(64) + 1])
    first = turn(np.arange(128)[:, None] * order[None, :], 128)
    tables["first"] = split_table(np.concatenate([first.real, first.imag], axis=1))
    back = np.conj(first).T
    tables["first_back"] = split_table(np.concatenate([back.real, back.imag], axis=1))
    chip_turn = turn(np.arange(64)[:, None] * np.arange(128)[None, :], 8192)
    tables["chip_turn"] = np.stack([chip_turn.real, chip_turn.imag]).astype(np.float32)
    base = []
    for core in range(2):
        blocks = []
        for zh in range(4):
            halves = []
            for half in range(2):
                q = 32 * (core if half == 0 else 1 - core) + np.arange(32)
                klow = np.arange(4)
                m = np.arange(64)
                power = (
                    m[:, None, None] * q[None, None, :] * 8
                    + zh * klow[None, :, None] * 128
                    + core * klow[None, :, None] * 64
                )
                halves.append(expanded(turn(power, 512).reshape(64, 128)))
            blocks.append(np.concatenate(halves, axis=1))
        base.append(np.concatenate(blocks, axis=0))
    tables["base"] = np.stack(base).astype(np.float32)
    index = np.arange(256)
    y, zl, x, l = index // 64, index // 32 % 2, index // 8 % 4, index % 8
    n = 64 * y + 16 * x + 8 * zl + l
    last = turn(n[:, None] * n[None, :], 256)
    for name, sign in (("last", 1.0), ("last_back", -1.0)):
        whole = np.block([[last.real, -sign * last.imag], [sign * last.imag, last.real]])
        blocks = whole.reshape(2, 4, 64, 512).transpose(1, 0, 2, 3).reshape(4, 128, 512)
        tables[name] = split_table(blocks)
    klow = np.arange(128) // 32
    twiddle = np.stack([turn(n[:, None] * (klow[None, :] + 4 * k2), 2048) for k2 in range(2)]) / 4096.0
    tables["twiddle"] = np.stack([twiddle.real, twiddle.imag], axis=1).astype(np.float32)
    return tables


TABLES = (
    "col_chirp",
    "row_chirp",
    "first",
    "first_back",
    "chip_turn",
    "base",
    "last",
    "last_back",
    "twiddle",
)


def split(value):
    high = value.astype(BF16)
    low = (value - high.astype(F32)).astype(BF16)
    return high, low


def dot(left, right):
    return jnp.dot(left, right, preferred_element_type=F32)


def dot_t(left, right):
    return lax.dot_general(left, right, (((1,), (1,)), ((), ())), preferred_element_type=F32)


def three(op, left, right):
    return op(left[0], right[0]) + (op(left[0], right[1]) + op(left[1], right[0]))


def device_of(chip, core):
    z = chip // 4 % 8
    return (z // 2) * 2 + core, (chip // 32) * 8 + (chip % 4) * 2 + z % 2


def flip(chip, offset):
    return chip ^ offset


def tile(ref, index):
    return ref.at[pl.ds(pl.multiple_of(index * 8, 8), 8)]


def kernel(
    row_off,
    col_off,
    obj_hbm,
    probe_hbm,
    int_hbm,
    col_chirp_hbm,
    row_chirp_hbm,
    first_hbm,
    first_back_hbm,
    chip_turn_hbm,
    base_hbm,
    last_hbm,
    last_back_hbm,
    twiddle_hbm,
    out_ref,
    obj,
    probe,
    inten,
    col_chirp,
    row_chirp,
    first,
    first_back,
    chip_turn,
    base,
    last,
    last_back,
    twiddle,
    rolled,
    arrived,
    wave,
    turned,
    field_out,
    field_in,
    mixed,
    mix_out,
    mix_in,
    mix_kept,
    data,
    again,
    factor,
    spread,
    shades_out,
    shades_in,
    back_out,
    back_in,
    part_out,
    part_in,
    part_own,
    peak_own,
    peak_z,
    peak_y,
    peak_x,
    peak_c,
    load_sem,
    shift_sem,
    int_sem,
    z_sem,
    y_sem,
    x_sem,
    c_sem,
    shade_sem,
    pass_sem,
    field_sem,
    mix_sem,
    part_sem,
    back_sem,
    local_sem,
    gates,
):
    outer, inner = lax.axis_index("outer"), lax.axis_index("inner")
    zh, core = outer // 2, outer % 2
    other = 1 - core
    z, y, x = zh * 2 + inner % 2, inner // 8, inner // 2 % 4
    chip = y * 32 + z * 4 + x
    number = outer * 32 + inner
    after, before = (number + 1) % 256, (number + 255) % 256
    sibling = device_of(chip, other)
    next_device = (after // 32, after % 32)
    last_device = (before // 32, before % 32)

    loads = []
    pairs = (
        (obj_hbm, obj),
        (probe_hbm, probe),
        (int_hbm, inten.at[core]),
        (base_hbm.at[core], base),
        (chip_turn_hbm, chip_turn),
        (col_chirp_hbm, col_chirp),
        (row_chirp_hbm, row_chirp),
        (first_hbm, first),
        (last_hbm, last),
        (last_back_hbm, last_back),
        (twiddle_hbm, twiddle),
        (first_back_hbm, first_back),
    )
    for slot, (source, target) in enumerate(pairs):
        copy = pltpu.make_async_copy(source, target, load_sem.at[slot])
        copy.start()
        loads.append(copy)

    barrier = pltpu.get_barrier_semaphore()

    def at_chip(dz, dy, dx):
        to = (y + dy + 4) % 4 * 32 + (z + dz + 8) % 8 * 4 + (x + dx + 4) % 4
        return device_of(to, core)

    around = [at_chip(*by) for by in ((1, 0, 0), (-1, 0, 0), (0, 1, 0), (0, -1, 0), (0, 0, 1), (0, 0, -1))]
    greeted = around + [sibling, next_device, last_device]
    for device in greeted:
        pl.semaphore_signal(barrier, inc=1, device_id=device, device_id_type=MESH)

    def tell(gate, devices):
        for device in devices:
            pl.semaphore_signal(gate, inc=1, device_id=device, device_id_type=MESH)


    rows_by, cols_by = row_off[0], col_off[0]
    tiles_by, lanes_by = cols_by // 128, cols_by % 128
    lane = lax.broadcasted_iota(jnp.int32, (8, 128), 1)
    sub = lax.broadcasted_iota(jnp.int32, (8, 128), 0)
    loads[0].wait()
    for part in range(2):
        for row in (7,):
            arrived[pl.ds(part * 512 + row * 64, 64), :] = jnp.zeros((64, 128), F32)
    wide_lane = lax.broadcasted_iota(jnp.int32, (64, 128), 1)
    shifts = []
    for part in range(2):

        def roll_step(step, carry, part=part):
            for inside in range(8):
                at = step * 8 + inside
                piece = obj[part, :, pl.ds(pl.multiple_of(at * 128, 128), 128)]
                moved = pltpu.roll(pltpu.roll(piece, lanes_by, 1), rows_by, 0)
                rolled[pl.ds(part * 512 + at, 8, stride=64), :] = moved
            return carry

        def tile_step(row, carry, part=part):
            at = pl.ds(pl.multiple_of(part * 512 + row * 64, 64), 64)
            moved = pltpu.roll(rolled[at, :], tiles_by, 0)
            rolled[at, :] = jnp.where(wide_lane < lanes_by, pltpu.roll(moved, 1, 0), moved)
            return carry

        lax.fori_loop(0, 8, roll_step, 0)
        lax.fori_loop(0, 8, tile_step, 0)
        if part == 0:
            pl.semaphore_wait(barrier, 9)
            tell(gates.at[0], around)
        shift = pltpu.make_async_remote_copy(
            src_ref=rolled.at[pl.ds(part * 512, 448)],
            dst_ref=arrived.at[pl.ds(part * 512, 448)],
            send_sem=shift_sem.at[part],
            recv_sem=shift_sem.at[2 + part],
            device_id=next_device,
            device_id_type=MESH,
        )
        shift.start()
        shifts.append(shift)
    loads[2].wait()
    share = pltpu.make_async_remote_copy(
        src_ref=inten.at[core],
        dst_ref=inten.at[core],
        send_sem=int_sem.at[0],
        recv_sem=int_sem.at[1],
        device_id=sibling,
        device_id_type=MESH,
    )
    share.start()
    pl.semaphore_wait(gates.at[0], 6)
    tell(gates.at[1], [at_chip(2, 0, 0), at_chip(-2, 0, 0)])

    loads[1].wait()

    def peak_step(step, best):
        for inside in range(8):
            at = pl.ds(pl.multiple_of((step * 8 + inside) * 128, 128), 128)
            real, imag = probe[0, :, at], probe[1, :, at]
            best = jnp.maximum(best, real * real + imag * imag)
        return best

    peak_own[0] = lax.fori_loop(0, 8, peak_step, jnp.zeros((8, 128), F32))

    pl.semaphore_wait(gates.at[1], 2)
    tell(gates.at[2], [device_of(flip(chip, k << 5), core) for k in range(1, 4)])
    loads[3].wait()
    loads[4].wait()
    chip_lane = lax.broadcasted_iota(jnp.int32, (64, 128), 1) == chip
    turn_re = jnp.sum(jnp.where(chip_lane, chip_turn[0], 0.0), axis=1, keepdims=True)
    turn_im = jnp.sum(jnp.where(chip_lane, chip_turn[1], 0.0), axis=1, keepdims=True)
    for block in range(4):
        low, high = pl.ds(block * 128, 64), pl.ds(block * 128 + 64, 64)
        for_re, for_im = base[low, :], base[high, :]
        for at, value in (
            (low, for_re * turn_re + for_im * turn_im),
            (high, for_im * turn_re - for_re * turn_im),
        ):
            high_part, low_part = split(value)
            mixed[0, at, :] = high_part
            mixed[1, at, :] = low_part

    pl.semaphore_wait(gates.at[2], 3)
    tell(gates.at[3], [device_of(flip(chip, k), core) for k in range(1, 4)])
    share.wait_recv()
    for c in range(2):

        def spread_step(step, carry, c=c):
            for inside in range(8):
                at = step * 8 + inside
                piece = inten[c, :, pl.ds(pl.multiple_of(at * 128, 128), 128)]
                spread[pl.ds(c * 64 + at, 8, stride=128), :] = piece
            return carry

        lax.fori_loop(0, 8, spread_step, 0)
    for l in range(4):
        shades_out[pl.ds(l, 128, stride=8), :] = jnp.transpose(spread[pl.ds(l * 128, 128), :])

    for l in range(4, 8):
        shades_out[pl.ds(l, 128, stride=8), :] = jnp.transpose(spread[pl.ds(l * 128, 128), :])
    pl.semaphore_wait(gates.at[3], 3)

    def send_shades(group):
        def shade_step(step, carry):
            target = flip(chip, group * 32 + step % 8 * 4 + step // 8 * 2 + core)
            pltpu.make_async_remote_copy(
                src_ref=tile(shades_out, target),
                dst_ref=shades_in.at[chip // 2, chip % 2],
                send_sem=shade_sem.at[0],
                recv_sem=shade_sem.at[1 + group],
                device_id=device_of(target, core),
                device_id_type=MESH,
            ).start()
            return carry

        lax.fori_loop(1 if group == 0 else 0, 16, shade_step, 0)
        if group == 0:

            @pl.when(core == 1)
            def _():
                shade_step(0, 0)

            @pl.when(core == 0)
            def _():
                own = pltpu.make_async_copy(
                    tile(shades_out, chip), shades_in.at[chip // 2, chip % 2], local_sem.at[0]
                )
                own.start()
                own.wait()

    for group in range(EARLY):
        send_shades(group)

    for slot in (5, 6, 7):
        loads[slot].wait()
    number_lane = lax.broadcasted_iota(jnp.int32, (8, 256), 1) == number
    row_re = jnp.sum(jnp.where(number_lane, row_chirp[0], 0.0), axis=1, keepdims=True)
    row_im = jnp.sum(jnp.where(number_lane, row_chirp[1], 0.0), axis=1, keepdims=True)

    def chirp_at(at):
        col_re, col_im = col_chirp[0, :, at], col_chirp[1, :, at]
        return row_re * col_re - row_im * col_im, row_re * col_im + row_im * col_re

    for shift in shifts:
        shift.wait_recv()

    def wave_step(step, carry):
        for inside in range(8):
            index = step * 8 + inside
            at = pl.ds(pl.multiple_of(index * 128, 128), 128)
            views = []
            for part in range(2):
                rows = pl.ds(part * 512 + index, 8, stride=64)
                views.append(jnp.where(sub < rows_by, arrived[rows, :], rolled[rows, :]))
            probe_re, probe_im = probe[0, :, at], probe[1, :, at]
            real = probe_re * views[0] - probe_im * views[1]
            imag = probe_re * views[1] + probe_im * views[0]
            wave[0, :, at] = real
            wave[1, :, at] = imag
            chirp_re, chirp_im = chirp_at(at)
            real, imag = real * chirp_re - imag * chirp_im, real * chirp_im + imag * chirp_re
            even = jnp.where(lane < 64, real, pltpu.roll(imag, 64, 1))
            odd = jnp.where(lane < 64, pltpu.roll(real, 64, 1), imag)
            turned[pl.ds(index, 8, stride=128), :] = even
            turned[pl.ds(64 + index, 8, stride=128), :] = odd
        return carry

    lax.fori_loop(0, 8, wave_step, 0)

    def times_i(value):
        half = lax.broadcasted_iota(jnp.int32, value.shape, 1) < 64
        moved = pltpu.roll(value, 64, 1)
        return jnp.where(half, -moved, moved)

    def first_step(load, table, store):
        for pair in range(4):
            sides = []
            for row in (2 * pair, 2 * pair + 1):
                value = load(row)
                sides.append(jnp.concatenate([value, times_i(value)], axis=0))
            result = three(dot, (table[0], table[1]), split(jnp.concatenate(sides, axis=1)))
            store(2 * pair, result[:, :128])
            store(2 * pair + 1, result[:, 128:])

    def store_field(row, value):
        field_out[pl.ds(row, 128, stride=8), :] = value

    first_step(lambda row: turned[pl.ds(row * 128, 128), :], first, store_field)

    def send_group(source, target, sem, group):
        def send_step(step, carry):
            to = flip(chip, group * 32 + step % 8 * 4 + step // 8)
            pltpu.make_async_remote_copy(
                src_ref=tile(source, to),
                dst_ref=tile(target, chip),
                send_sem=sem.at[0],
                recv_sem=sem.at[1 + group],
                device_id=device_of(to, core),
                device_id_type=MESH,
            ).start()
            return carry

        lax.fori_loop(1 if group == 0 else 0, 32, send_step, 0)
        if group == 0:
            own = pltpu.make_async_copy(tile(source, chip), tile(target, chip), local_sem.at[0])
            own.start()
            own.wait()

    def all_of(source, target, sem, rows, group=0):
        return pltpu.make_async_remote_copy(
            src_ref=source.at[pl.ds(0, rows)],
            dst_ref=target.at[pl.ds(0, rows)],
            send_sem=sem.at[0],
            recv_sem=sem.at[1 + group],
            device_id=sibling,
            device_id_type=MESH,
        )

    def got_group(source, target, sem, group):
        all_of(source, target, sem, 248 if group == 0 else 256, group).wait_recv()

    for group in range(4):
        send_group(field_out, field_in, field_sem, group)
    for group in range(EARLY, 4):
        send_shades(group)

    def peak_line(source, target, sem, count, by):
        copies = []
        for k in range(1, count):
            copy = pltpu.make_async_remote_copy(
                src_ref=source,
                dst_ref=target.at[k - 1],
                send_sem=sem.at[k - 1],
                recv_sem=sem.at[count - 2 + k],
                device_id=device_of(flip(chip, k << by), core),
                device_id_type=MESH,
            )
            copy.start()
            copies.append(copy)
        return copies

    z_line = peak_line(peak_own.at[0], peak_z, z_sem, 8, 2)


    mine = (chip + core) % 2

    def pass_shades(group):
        if group == 0:

            @pl.when(core == 0)
            def _():
                all_of(shades_out, field_in, shade_sem, 120, group).wait_recv()

            @pl.when(core == 1)
            def _():
                all_of(shades_out, field_in, shade_sem, 128, group).wait_recv()

        else:
            all_of(shades_out, field_in, shade_sem, 128, group).wait_recv()
        block = pl.ds((y ^ group) * 16, 16)
        copy = pltpu.make_async_remote_copy(
            src_ref=shades_in.at[block, mine],
            dst_ref=shades_in.at[block, mine],
            send_sem=pass_sem.at[group],
            recv_sem=pass_sem.at[4 + group],
            device_id=sibling,
            device_id_type=MESH,
        )
        copy.start()
        return copy

    lane_group = lax.broadcasted_iota(jnp.int32, (64, 128), 1) // 32

    def make_factor(group):
        for c in range(2):
            shade = jnp.zeros((64, 128), F32)
            for digit in range(4):
                want = 2 * (digit % 2) + digit // 2
                by = (32 * (want - 2 * c - core) + 128) % 128
                part = shades_in[pl.ds((y ^ group) * 16 + digit * 4, 4)].reshape(64, 128)
                shade = jnp.where(lane_group == want, pltpu.roll(part, by, 1), shade)
            factor[c, pl.ds(pl.multiple_of((y ^ group) * 64, 64), 64), :] = jnp.sqrt(shade)

    passes = [pass_shades(group) for group in range(EARLY)]
    for group in range(EARLY):
        passes[group].wait()
        make_factor(group)

    sent_half = (mixed.at[0, :, pl.ds(256, 256)], mixed.at[1, :, pl.ds(256, 256)])
    kept_half = (mixed.at[0, :, pl.ds(0, 256)], mixed.at[1, :, pl.ds(0, 256)])
    mixes = []
    sign = jnp.where(core == 0, 1.0, -1.0).astype(F32)
    loads[8].wait()
    loads[10].wait()

    def prepare(group):
        mixes[group].wait_recv()
        here = y ^ group
        rows = pl.ds(pl.multiple_of(here * 64, 64), 64)
        kept, got = mix_kept[rows, :], mix_in[rows, :]
        for k2, total in enumerate((kept + got, (kept - got) * sign)):
            real, imag = total[:, :128], total[:, 128:]
            turn_r, turn_i = twiddle[k2, 0, rows, :], twiddle[k2, 1, rows, :]
            lanes = pl.ds(k2 * 128, 128)
            for ri, value in enumerate(
                (real * turn_r - imag * turn_i, real * turn_i + imag * turn_r)
            ):
                at = pl.ds(pl.multiple_of(ri * 256 + here * 64, 64), 64)
                high_part, low_part = split(value)
                data[0, at, lanes] = high_part
                data[1, at, lanes] = low_part

    for group in range(4):
        got_group(field_out, field_in, field_sem, group)
        here = y ^ group
        pieces = [field_in[pl.ds(pl.multiple_of(here * 256 + digit * 64, 64), 64), :] for digit in range(4)]
        joined = split(jnp.concatenate(pieces, axis=1))
        rows = pl.ds(pl.multiple_of(here * 64, 64), 64)
        mix_out[rows, :] = three(dot, joined, (sent_half[0][...], sent_half[1][...]))
        mix = pltpu.make_async_remote_copy(
            src_ref=mix_out.at[rows],
            dst_ref=mix_in.at[rows],
            send_sem=mix_sem.at[group],
            recv_sem=mix_sem.at[4 + group],
            device_id=sibling,
            device_id_type=MESH,
        )
        mix.start()
        mixes.append(mix)
        mix_kept[rows, :] = three(dot, joined, (kept_half[0][...], kept_half[1][...]))
        if group > 0:
            prepare(group - 1)
    for copy in z_line:
        copy.wait_recv()
    best = peak_own[0]
    for k in range(7):
        best = jnp.maximum(best, peak_z[k])
    peak_own[1] = best
    y_line = peak_line(peak_own.at[1], peak_y, y_sem, 4, 5)
    late = [pass_shades(group) for group in range(EARLY, 4)]
    prepare(3)
    for group in range(EARLY, 4):
        late[group - EARLY].wait()
        make_factor(group)
    for block in range(4):
        value = three(dot, (last[0, block], last[1, block]), (data[0], data[1]))
        rows = pl.ds(block * 64, 64)
        for k2 in range(2):
            lanes = pl.ds(k2 * 128, 128)
            real = value[:64, k2 * 128 : (k2 + 1) * 128]
            imag = value[64:, k2 * 128 : (k2 + 1) * 128]
            size = jnp.sqrt(real * real + imag * imag)
            scale = factor[k2, rows, :] / jnp.maximum(size, FLOOR_LEVEL)
            for ri, part in enumerate((real * scale, imag * scale)):
                high_part, low_part = split(part)
                again[0, pl.ds(ri * 256 + block * 64, 64), lanes] = high_part
                again[1, pl.ds(ri * 256 + block * 64, 64), lanes] = low_part
    loads[9].wait()
    own_core = core == 0
    swaps = []
    for half in range(2):
        for group in (2 * half, 2 * half + 1):
            here = y ^ group
            rows = pl.ds(pl.multiple_of(here * 64, 64), 64)
            value = three(dot, (last_back[0, here], last_back[1, here]), (again[0], again[1]))
            parts = []
            for k2 in range(2):
                real = value[:64, k2 * 128 : (k2 + 1) * 128]
                imag = value[64:, k2 * 128 : (k2 + 1) * 128]
                turn_r, turn_i = twiddle[k2, 0, rows, :], twiddle[k2, 1, rows, :]
                parts.append(
                    jnp.concatenate(
                        [real * turn_r + imag * turn_i, imag * turn_r - real * turn_i], axis=1
                    )
                )
            plus, minus = parts[0] + parts[1], parts[0] - parts[1]
            part_out[rows, :] = jnp.where(own_core, minus, plus)
            part_own[rows, :] = jnp.where(own_core, plus, minus)
        rows = pl.ds(pl.multiple_of((y // 2 ^ half) * 128, 128), 128)
        swap = pltpu.make_async_remote_copy(
            src_ref=part_out.at[rows],
            dst_ref=part_in.at[rows],
            send_sem=part_sem.at[half],
            recv_sem=part_sem.at[2 + half],
            device_id=sibling,
            device_id_type=MESH,
        )
        swap.start()
        swaps.append(swap)
    for copy in y_line:
        copy.wait_recv()
    for k in range(3):
        best = jnp.maximum(best, peak_y[k])
    peak_own[2] = best
    x_line = peak_line(peak_own.at[2], peak_x, x_sem, 4, 0)
    for half in range(2):
        swaps[half].wait_recv()
        rows = pl.ds(pl.multiple_of((y // 2 ^ half) * 128, 128), 128)
        joined = split(jnp.concatenate([part_own[rows, :], part_in[rows, :]], axis=1))
        result = three(dot_t, joined, (mixed[0], mixed[1]))
        for low in range(2):
            for digit in range(4):
                at = pl.multiple_of((y // 2 ^ half) * 512 + low * 256 + digit * 64, 64)
                back_out[pl.ds(at, 64), :] = result[low * 64 : (low + 1) * 64, digit * 128 : (digit + 1) * 128]
        for group in (2 * half, 2 * half + 1):
            send_group(back_out, back_in, back_sem, group)
    for copy in x_line:
        copy.wait_recv()
    for k in range(3):
        best = jnp.maximum(best, peak_x[k])
    peak_own[3] = best
    c_line = pltpu.make_async_remote_copy(
        src_ref=peak_own.at[3],
        dst_ref=peak_c,
        send_sem=c_sem.at[0],
        recv_sem=c_sem.at[1],
        device_id=sibling,
        device_id_type=MESH,
    )
    c_line.start()
    c_line.wait_recv()
    gain = 1.0 / jnp.max(jnp.maximum(best, peak_c[...]))

    loads[11].wait()
    for group in range(4):
        got_group(back_out, back_in, back_sem, group)

    def store_turned(row, value):
        turned[pl.ds(row * 128, 128), :] = value

    first_step(lambda row: back_in[pl.ds(row, 128, stride=8), :], first_back, store_turned)

    def last_step(step, carry):
        for inside in range(8):
            index = step * 8 + inside
            at = pl.ds(pl.multiple_of(index * 128, 128), 128)
            even = turned[pl.ds(index, 8, stride=128), :]
            odd = turned[pl.ds(64 + index, 8, stride=128), :]
            real = jnp.where(lane < 64, even, pltpu.roll(odd, 64, 1))
            imag = jnp.where(lane < 64, pltpu.roll(even, 64, 1), odd)
            chirp_re, chirp_im = chirp_at(at)
            step_re = real * chirp_re + imag * chirp_im - wave[0, :, at]
            step_im = imag * chirp_re - real * chirp_im - wave[1, :, at]
            probe_re, probe_im = probe[0, :, at], probe[1, :, at]
            out_ref[0, :, at] = (probe_re * step_re + probe_im * step_im) * gain
            out_ref[1, :, at] = (probe_re * step_im - probe_im * step_re) * gain
        return carry

    lax.fori_loop(0, 8, last_step, 0)

    for shift in shifts:
        shift.wait_send()
    share.wait_send()
    for copy in z_line + y_line + x_line + mixes + swaps:
        copy.wait_send()
    c_line.wait_send()
    all_of(field_out, field_in, field_sem, 1016).wait_send()
    all_of(back_out, back_in, back_sem, 1016).wait_send()

    @pl.when(core == 0)
    def _():
        all_of(shades_out, field_in, shade_sem, 504).wait_send()

    @pl.when(core == 1)
    def _():
        all_of(shades_out, field_in, shade_sem, 512).wait_send()


def body(object_field, probe, intensity, row_offset, col_offset):
    tables = make_tables()
    constants = [jnp.asarray(tables[name]) for name in TABLES]
    vmem, dma = pltpu.VMEM, pltpu.SemaphoreType.DMA
    anywhere = pl.BlockSpec(memory_space=pltpu.HBM)
    scalar = pl.BlockSpec(memory_space=pltpu.SMEM)
    inside = pl.BlockSpec(memory_space=pltpu.VMEM)
    state = vmem((1024, 128), F32)
    scratch = [
        vmem((2, 8, 8192), F32),
        vmem((2, 8, 8192), F32),
        vmem((2, 8, 8192), F32),
        vmem((2, 1, 8192), F32),
        vmem((2, 8, 256), F32),
        vmem((2, 128, 256), BF16),
        vmem((2, 128, 256), BF16),
        vmem((2, 64, 128), F32),
        vmem((512, 512), F32),
        vmem((2, 4, 128, 512), BF16),
        vmem((2, 4, 128, 512), BF16),
        vmem((2, 2, 256, 128), F32),
        state,
        state,
        vmem((2, 8, 8192), F32),
        state,
        state,
        state,
        vmem((2, 512, 512), BF16),
        vmem((256, 256), F32),
        vmem((256, 256), F32),
        vmem((256, 256), F32),
        vmem((2, 512, 256), BF16),
        vmem((2, 512, 256), BF16),
        vmem((2, 256, 128), F32),
        state,
        state,
        vmem((64, 2, 8, 128), F32),
        state,
        state,
        vmem((256, 256), F32),
        vmem((256, 256), F32),
        vmem((256, 256), F32),
        vmem((4, 8, 128), F32),
        vmem((7, 8, 128), F32),
        vmem((3, 8, 128), F32),
        vmem((3, 8, 128), F32),
        vmem((8, 128), F32),
        dma((12,)),
        dma((4,)),
        dma((2,)),
        dma((14,)),
        dma((6,)),
        dma((6,)),
        dma((2,)),
        dma((5,)),
        dma((8,)),
        dma((5,)),
        dma((8,)),
        dma((4,)),
        dma((5,)),
        dma((1,)),
        pltpu.SemaphoreType.REGULAR((4,)),
    ]
    return pl.pallas_call(
        kernel,
        out_shape=jax.ShapeDtypeStruct(object_field.shape, F32),
        in_specs=[scalar, scalar] + [anywhere] * (3 + len(constants)),
        out_specs=inside,
        scratch_shapes=scratch,
        compiler_params=pltpu.CompilerParams(
            collective_id=0, has_side_effects=True, vmem_limit_bytes=60 << 20
        ),
        cost_estimate=pl.CostEstimate(
            flops=2_000_000_000, bytes_accessed=8_000_000, transcendentals=200_000
        ),
    )(row_offset, col_offset, object_field, probe, intensity, *constants)


def solution(mesh):
    placed = (
        P(None, ("outer", "inner"), None),
        P(None, ("outer", "inner"), None),
        P(("outer", "inner"), None),
        P(),
        P(),
    )
    return jax.shard_map(
        body,
        mesh=mesh,
        in_specs=placed,
        out_specs=P(None, ("outer", "inner"), None),
        check_vma=False,
    )
```

```python
import math

import jax
import jax.numpy as jnp
import numpy as np
from jax import lax
from jax.experimental import pallas as pl
from jax.experimental.pallas import tpu as pltpu
from jax.sharding import PartitionSpec as P

FLOOR_LEVEL = 0.1
MESH = pl.DeviceIdType.MESH
CHIPS = 128
F32 = jnp.float32
BF16 = jnp.bfloat16


def split_table(table):
    table = np.asarray(table, np.float64).astype(np.float32)
    high = table.astype(jnp.bfloat16)
    low = (table - high.astype(np.float32)).astype(jnp.bfloat16)
    return np.stack([high, low])


def turn(numerator, modulus):
    angle = -2.0 * np.pi * (np.asarray(numerator) % modulus) / modulus
    return np.exp(1j * angle)


def expanded(table):
    return np.block([[table.real, table.imag], [-table.imag, table.real]])


def make_tables():
    tables = {}
    col = np.arange(8192, dtype=np.int64) - 4096
    col_phase = np.pi / 8192 * (col * col % 16384)
    tables["col_chirp"] = np.stack([np.cos(col_phase), np.sin(col_phase)]).reshape(2, 1, 8192).astype(np.float32)
    row = np.arange(2048, dtype=np.int64) - 1024
    row_phase = (np.pi / 2048 * (row * row % 4096)).reshape(256, 8).T
    tables["row_chirp"] = np.stack([np.cos(row_phase), np.sin(row_phase)]).astype(np.float32)
    order = np.concatenate([2 * np.arange(64), 2 * np.arange(64) + 1])
    first = turn(np.arange(128)[:, None] * order[None, :], 128)
    tables["first"] = split_table(np.concatenate([first.real, first.imag], axis=1))
    back = np.conj(first).T
    tables["first_back"] = split_table(np.concatenate([back.real, back.imag], axis=1))
    chip_turn = turn(np.arange(64)[:, None] * np.arange(128)[None, :], 8192)
    tables["chip_turn"] = np.stack([chip_turn.real, chip_turn.imag]).astype(np.float32)
    base = []
    for core in range(2):
        blocks = []
        for zh in range(4):
            halves = []
            for half in range(2):
                q = 32 * (core if half == 0 else 1 - core) + np.arange(32)
                klow = np.arange(4)
                m = np.arange(64)
                power = (
                    m[:, None, None] * q[None, None, :] * 8
                    + zh * klow[None, :, None] * 128
                    + core * klow[None, :, None] * 64
                )
                halves.append(expanded(turn(power, 512).reshape(64, 128)))
            blocks.append(np.concatenate(halves, axis=1))
        base.append(np.concatenate(blocks, axis=0))
    tables["base"] = np.stack(base).astype(np.float32)
    index = np.arange(256)
    y, zl, x, l = index // 64, index // 32 % 2, index // 8 % 4, index % 8
    n = 64 * y + 16 * x + 8 * zl + l
    last = turn(n[:, None] * n[None, :], 256)
    for name, sign in (("last", 1.0), ("last_back", -1.0)):
        whole = np.block([[last.real, -sign * last.imag], [sign * last.imag, last.real]])
        blocks = whole.reshape(2, 4, 64, 512).transpose(1, 0, 2, 3).reshape(4, 128, 512)
        tables[name] = split_table(blocks)
    klow = np.arange(128) // 32
    twiddle = np.stack([turn(n[:, None] * (klow[None, :] + 4 * k2), 2048) for k2 in range(2)]) / 4096.0
    tables["twiddle"] = np.stack([twiddle.real, twiddle.imag], axis=1).astype(np.float32)
    return tables


TABLES = (
    "col_chirp",
    "row_chirp",
    "first",
    "first_back",
    "chip_turn",
    "base",
    "last",
    "last_back",
    "twiddle",
)


def split(value):
    high = value.astype(BF16)
    low = (value - high.astype(F32)).astype(BF16)
    return high, low


def dot(left, right):
    return jnp.dot(left, right, preferred_element_type=F32)


def dot_t(left, right):
    return lax.dot_general(left, right, (((1,), (1,)), ((), ())), preferred_element_type=F32)


def three(op, left, right):
    return op(left[0], right[0]) + (op(left[0], right[1]) + op(left[1], right[0]))


def device_of(chip, core):
    z = chip // 4 % 8
    return (z // 2) * 2 + core, (chip // 32) * 8 + (chip % 4) * 2 + z % 2


def flip(chip, offset):
    return chip ^ offset


def tile(ref, index):
    return ref.at[pl.ds(pl.multiple_of(index * 8, 8), 8)]


def kernel(
    row_off,
    col_off,
    obj_hbm,
    probe_hbm,
    int_hbm,
    col_chirp_hbm,
    row_chirp_hbm,
    first_hbm,
    first_back_hbm,
    chip_turn_hbm,
    base_hbm,
    last_hbm,
    last_back_hbm,
    twiddle_hbm,
    out_ref,
    obj,
    probe,
    inten,
    col_chirp,
    row_chirp,
    first,
    first_back,
    chip_turn,
    base,
    last,
    last_back,
    twiddle,
    rolled,
    arrived,
    wave,
    turned,
    field_out,
    field_in,
    mixed,
    mix_out,
    mix_in,
    mix_kept,
    data,
    again,
    factor,
    spread,
    shades_out,
    shades_in,
    back_out,
    back_in,
    part_out,
    part_in,
    part_own,
    peak_own,
    peak_z,
    peak_y,
    peak_x,
    peak_c,
    load_sem,
    shift_sem,
    int_sem,
    z_sem,
    y_sem,
    x_sem,
    c_sem,
    shade_sem,
    pass_sem,
    field_sem,
    mix_sem,
    part_sem,
    back_sem,
    local_sem,
    gates,
):
    outer, inner = lax.axis_index("outer"), lax.axis_index("inner")
    zh, core = outer // 2, outer % 2
    other = 1 - core
    z, y, x = zh * 2 + inner % 2, inner // 8, inner // 2 % 4
    chip = y * 32 + z * 4 + x
    number = outer * 32 + inner
    after, before = (number + 1) % 256, (number + 255) % 256
    sibling = device_of(chip, other)
    next_device = (after // 32, after % 32)
    last_device = (before // 32, before % 32)

    loads = []
    pairs = (
        (obj_hbm.at[0], obj.at[0]),
        (probe_hbm, probe),
        (int_hbm, inten.at[core]),
        (base_hbm.at[core], base),
        (chip_turn_hbm, chip_turn),
        (col_chirp_hbm, col_chirp),
        (row_chirp_hbm, row_chirp),
        (first_hbm, first),
        (last_hbm, last),
        (last_back_hbm, last_back),
        (twiddle_hbm, twiddle),
        (first_back_hbm, first_back),
        (obj_hbm.at[1], obj.at[1]),
    )
    for slot, (source, target) in enumerate(pairs):
        loads.append(pltpu.make_async_copy(source, target, load_sem.at[slot]))
    for slot in (0, 2, 12):
        loads[slot].start()

    barrier = pltpu.get_barrier_semaphore()

    def at_chip(dz, dy, dx):
        to = (y + dy + 4) % 4 * 32 + (z + dz + 8) % 8 * 4 + (x + dx + 4) % 4
        return device_of(to, core)

    around = [at_chip(*by) for by in ((1, 0, 0), (-1, 0, 0), (0, 1, 0), (0, -1, 0), (0, 0, 1), (0, 0, -1))]
    greeted = around + [sibling, next_device, last_device]
    for device in greeted:
        pl.semaphore_signal(barrier, inc=1, device_id=device, device_id_type=MESH)

    def tell(gate, devices):
        for device in devices:
            pl.semaphore_signal(gate, inc=1, device_id=device, device_id_type=MESH)


    rows_by, cols_by = row_off[0], col_off[0]
    tiles_by, lanes_by = cols_by // 128, cols_by % 128
    lane = lax.broadcasted_iota(jnp.int32, (8, 128), 1)
    sub = lax.broadcasted_iota(jnp.int32, (8, 128), 0)
    for part in range(2):
        for row in (7,):
            arrived[pl.ds(part * 512 + row * 64, 64), :] = jnp.zeros((64, 128), F32)
    wide_lane = lax.broadcasted_iota(jnp.int32, (64, 128), 1)
    shifts = []
    for part in range(2):

        def roll_step(step, carry, part=part):
            for inside in range(8):
                at = step * 8 + inside
                piece = obj[part, :, pl.ds(pl.multiple_of(at * 128, 128), 128)]
                moved = pltpu.roll(pltpu.roll(piece, lanes_by, 1), rows_by, 0)
                rolled[pl.ds(part * 512 + at, 8, stride=64), :] = moved
            return carry

        def tile_step(row, carry, part=part):
            at = pl.ds(pl.multiple_of(part * 512 + row * 64, 64), 64)
            moved = pltpu.roll(rolled[at, :], tiles_by, 0)
            rolled[at, :] = jnp.where(wide_lane < lanes_by, pltpu.roll(moved, 1, 0), moved)
            return carry

        loads[12 * part].wait()
        lax.fori_loop(0, 8, roll_step, 0)
        lax.fori_loop(0, 8, tile_step, 0)
        if part == 0:
            pl.semaphore_wait(barrier, 9)
            tell(gates.at[0], around)
        shift = pltpu.make_async_remote_copy(
            src_ref=rolled.at[pl.ds(part * 512, 448)],
            dst_ref=arrived.at[pl.ds(part * 512, 448)],
            send_sem=shift_sem.at[part],
            recv_sem=shift_sem.at[2 + part],
            device_id=next_device,
            device_id_type=MESH,
        )
        shift.start()
        shifts.append(shift)
        if part == 0:
            loads[2].wait()
            share = pltpu.make_async_remote_copy(
                src_ref=inten.at[core],
                dst_ref=inten.at[core],
                send_sem=int_sem.at[0],
                recv_sem=int_sem.at[1],
                device_id=sibling,
                device_id_type=MESH,
            )
            share.start()
    for slot in (1, 3, 4, 5, 6, 7, 8, 9, 10, 11):
        loads[slot].start()
    pl.semaphore_wait(gates.at[0], 6)
    tell(gates.at[1], [at_chip(2, 0, 0), at_chip(-2, 0, 0)])

    pl.semaphore_wait(gates.at[1], 2)
    tell(gates.at[2], [device_of(flip(chip, k << 5), core) for k in range(1, 4)])
    share.wait_recv()
    for c in range(2):

        def spread_step(step, carry, c=c):
            for inside in range(8):
                at = step * 8 + inside
                piece = inten[c, :, pl.ds(pl.multiple_of(at * 128, 128), 128)]
                spread[pl.ds(c * 64 + at, 8, stride=128), :] = piece
            return carry

        lax.fori_loop(0, 8, spread_step, 0)
    pl.semaphore_wait(gates.at[2], 3)
    tell(gates.at[3], [device_of(flip(chip, k), core) for k in range(1, 4)])
    for l in range(4):
        shades_out[pl.ds(l, 128, stride=8), :] = jnp.transpose(spread[pl.ds(l * 128, 128), :])

    for l in range(4, 8):
        shades_out[pl.ds(l, 128, stride=8), :] = jnp.transpose(spread[pl.ds(l * 128, 128), :])
    pl.semaphore_wait(gates.at[3], 3)

    def send_shades(group):
        def shade_step(step, carry):
            target = flip(chip, group * 32 + step % 8 * 4 + step // 8 * 2 + core)
            pltpu.make_async_remote_copy(
                src_ref=tile(shades_out, target),
                dst_ref=shades_in.at[chip // 2, chip % 2],
                send_sem=shade_sem.at[0],
                recv_sem=shade_sem.at[1 + group],
                device_id=device_of(target, core),
                device_id_type=MESH,
            ).start()
            return carry

        lax.fori_loop((1 - core) if group == 0 else 0, 16, shade_step, 0)

    for group in range(4):
        send_shades(group)

    @pl.when(core == 0)
    def _():
        own = pltpu.make_async_copy(
            tile(shades_out, chip), shades_in.at[chip // 2, chip % 2], local_sem.at[0]
        )
        own.start()
        own.wait()

    loads[1].wait()

    def peak_step(step, best):
        for inside in range(8):
            at = pl.ds(pl.multiple_of((step * 8 + inside) * 128, 128), 128)
            real, imag = probe[0, :, at], probe[1, :, at]
            best = jnp.maximum(best, real * real + imag * imag)
        return best

    peak_own[0] = lax.fori_loop(0, 8, peak_step, jnp.zeros((8, 128), F32))

    loads[3].wait()
    loads[4].wait()
    chip_lane = lax.broadcasted_iota(jnp.int32, (64, 128), 1) == chip
    turn_re = jnp.sum(jnp.where(chip_lane, chip_turn[0], 0.0), axis=1, keepdims=True)
    turn_im = jnp.sum(jnp.where(chip_lane, chip_turn[1], 0.0), axis=1, keepdims=True)
    for block in range(4):
        low, high = pl.ds(block * 128, 64), pl.ds(block * 128 + 64, 64)
        for_re, for_im = base[low, :], base[high, :]
        for at, value in (
            (low, for_re * turn_re + for_im * turn_im),
            (high, for_im * turn_re - for_re * turn_im),
        ):
            high_part, low_part = split(value)
            mixed[0, at, :] = high_part
            mixed[1, at, :] = low_part

    for slot in (5, 6, 7):
        loads[slot].wait()
    number_lane = lax.broadcasted_iota(jnp.int32, (8, 256), 1) == number
    row_re = jnp.sum(jnp.where(number_lane, row_chirp[0], 0.0), axis=1, keepdims=True)
    row_im = jnp.sum(jnp.where(number_lane, row_chirp[1], 0.0), axis=1, keepdims=True)

    def chirp_at(at):
        col_re, col_im = col_chirp[0, :, at], col_chirp[1, :, at]
        return row_re * col_re - row_im * col_im, row_re * col_im + row_im * col_re

    for shift in shifts:
        shift.wait_recv()

    def wave_step(step, carry):
        for inside in range(8):
            index = step * 8 + inside
            at = pl.ds(pl.multiple_of(index * 128, 128), 128)
            views = []
            for part in range(2):
                rows = pl.ds(part * 512 + index, 8, stride=64)
                views.append(jnp.where(sub < rows_by, arrived[rows, :], rolled[rows, :]))
            probe_re, probe_im = probe[0, :, at], probe[1, :, at]
            real = probe_re * views[0] - probe_im * views[1]
            imag = probe_re * views[1] + probe_im * views[0]
            wave[0, :, at] = real
            wave[1, :, at] = imag
            chirp_re, chirp_im = chirp_at(at)
            real, imag = real * chirp_re - imag * chirp_im, real * chirp_im + imag * chirp_re
            even = jnp.where(lane < 64, real, pltpu.roll(imag, 64, 1))
            odd = jnp.where(lane < 64, pltpu.roll(real, 64, 1), imag)
            turned[pl.ds(index, 8, stride=128), :] = even
            turned[pl.ds(64 + index, 8, stride=128), :] = odd
        return carry

    lax.fori_loop(0, 8, wave_step, 0)

    def times_i(value):
        half = lax.broadcasted_iota(jnp.int32, value.shape, 1) < 64
        moved = pltpu.roll(value, 64, 1)
        return jnp.where(half, -moved, moved)

    def first_step(load, table, store):
        for pair in range(4):
            sides = []
            for row in (2 * pair, 2 * pair + 1):
                value = load(row)
                sides.append(jnp.concatenate([value, times_i(value)], axis=0))
            result = three(dot, (table[0], table[1]), split(jnp.concatenate(sides, axis=1)))
            store(2 * pair, result[:, :128])
            store(2 * pair + 1, result[:, 128:])

    def store_field(row, value):
        field_out[pl.ds(row, 128, stride=8), :] = value

    first_step(lambda row: turned[pl.ds(row * 128, 128), :], first, store_field)

    def send_group(source, target, sem, group):
        def send_step(step, carry):
            to = flip(chip, group * 32 + step % 8 * 4 + step // 8)
            pltpu.make_async_remote_copy(
                src_ref=tile(source, to),
                dst_ref=tile(target, chip),
                send_sem=sem.at[0],
                recv_sem=sem.at[1 + group],
                device_id=device_of(to, core),
                device_id_type=MESH,
            ).start()
            return carry

        lax.fori_loop(1 if group == 0 else 0, 32, send_step, 0)

    def keep_own(source, target):
        own = pltpu.make_async_copy(tile(source, chip), tile(target, chip), local_sem.at[0])
        own.start()
        own.wait()

    def all_of(source, target, sem, rows, group=0):
        return pltpu.make_async_remote_copy(
            src_ref=source.at[pl.ds(0, rows)],
            dst_ref=target.at[pl.ds(0, rows)],
            send_sem=sem.at[0],
            recv_sem=sem.at[1 + group],
            device_id=sibling,
            device_id_type=MESH,
        )

    def got_group(source, target, sem, group):
        all_of(source, target, sem, 248 if group == 0 else 256, group).wait_recv()

    def peak_line(source, target, sem, count, by):
        copies = []
        for k in range(1, count):
            copy = pltpu.make_async_remote_copy(
                src_ref=source,
                dst_ref=target.at[k - 1],
                send_sem=sem.at[k - 1],
                recv_sem=sem.at[count - 2 + k],
                device_id=device_of(flip(chip, k << by), core),
                device_id_type=MESH,
            )
            copy.start()
            copies.append(copy)
        return copies

    z_line = peak_line(peak_own.at[0], peak_z, z_sem, 8, 2)
    for group in range(4):
        send_group(field_out, field_in, field_sem, group)
    keep_own(field_out, field_in)


    mine = (chip + core) % 2

    def pass_shades(group):
        if group == 0:

            @pl.when(core == 0)
            def _():
                all_of(shades_out, field_in, shade_sem, 120, group).wait_recv()

            @pl.when(core == 1)
            def _():
                all_of(shades_out, field_in, shade_sem, 128, group).wait_recv()

        else:
            all_of(shades_out, field_in, shade_sem, 128, group).wait_recv()
        block = pl.ds((y ^ group) * 16, 16)
        copy = pltpu.make_async_remote_copy(
            src_ref=shades_in.at[block, mine],
            dst_ref=shades_in.at[block, mine],
            send_sem=pass_sem.at[group],
            recv_sem=pass_sem.at[4 + group],
            device_id=sibling,
            device_id_type=MESH,
        )
        copy.start()
        return copy

    lane_group = lax.broadcasted_iota(jnp.int32, (64, 128), 1) // 32

    def make_factor(group):
        for c in range(2):
            shade = jnp.zeros((64, 128), F32)
            for digit in range(4):
                want = 2 * (digit % 2) + digit // 2
                by = (32 * (want - 2 * c - core) + 128) % 128
                part = shades_in[pl.ds((y ^ group) * 16 + digit * 4, 4)].reshape(64, 128)
                shade = jnp.where(lane_group == want, pltpu.roll(part, by, 1), shade)
            factor[c, pl.ds(pl.multiple_of((y ^ group) * 64, 64), 64), :] = jnp.sqrt(shade)

    for copy in z_line:
        copy.wait_recv()
    best = peak_own[0]
    for k in range(7):
        best = jnp.maximum(best, peak_z[k])
    peak_own[1] = best
    y_line = peak_line(peak_own.at[1], peak_y, y_sem, 4, 5)
    passes = [pass_shades(group) for group in range(4)]
    for copy in y_line:
        copy.wait_recv()
    for k in range(3):
        best = jnp.maximum(best, peak_y[k])
    peak_own[2] = best
    x_line = peak_line(peak_own.at[2], peak_x, x_sem, 4, 0)

    sent_half = (mixed.at[0, :, pl.ds(256, 256)], mixed.at[1, :, pl.ds(256, 256)])
    kept_half = (mixed.at[0, :, pl.ds(0, 256)], mixed.at[1, :, pl.ds(0, 256)])
    mixes = []
    sign = jnp.where(core == 0, 1.0, -1.0).astype(F32)
    loads[8].wait()
    loads[10].wait()

    def prepare(group):
        mixes[group].wait_recv()
        here = y ^ group
        rows = pl.ds(pl.multiple_of(here * 64, 64), 64)
        kept, got = mix_kept[rows, :], mix_in[rows, :]
        for k2, total in enumerate((kept + got, (kept - got) * sign)):
            real, imag = total[:, :128], total[:, 128:]
            turn_r, turn_i = twiddle[k2, 0, rows, :], twiddle[k2, 1, rows, :]
            lanes = pl.ds(k2 * 128, 128)
            for ri, value in enumerate(
                (real * turn_r - imag * turn_i, real * turn_i + imag * turn_r)
            ):
                at = pl.ds(pl.multiple_of(ri * 256 + here * 64, 64), 64)
                high_part, low_part = split(value)
                data[0, at, lanes] = high_part
                data[1, at, lanes] = low_part

    for group in range(4):
        got_group(field_out, field_in, field_sem, group)
        here = y ^ group
        pieces = [field_in[pl.ds(pl.multiple_of(here * 256 + digit * 64, 64), 64), :] for digit in range(4)]
        joined = split(jnp.concatenate(pieces, axis=1))
        rows = pl.ds(pl.multiple_of(here * 64, 64), 64)
        mix_out[rows, :] = three(dot, joined, (sent_half[0][...], sent_half[1][...]))
        mix = pltpu.make_async_remote_copy(
            src_ref=mix_out.at[rows],
            dst_ref=mix_in.at[rows],
            send_sem=mix_sem.at[group],
            recv_sem=mix_sem.at[4 + group],
            device_id=sibling,
            device_id_type=MESH,
        )
        mix.start()
        mixes.append(mix)
        mix_kept[rows, :] = three(dot, joined, (kept_half[0][...], kept_half[1][...]))
        if group > 0:
            prepare(group - 1)
        else:
            for early in range(4):
                passes[early].wait()
                make_factor(early)
        if group == 1:
            for copy in x_line:
                copy.wait_recv()
            for k in range(3):
                best = jnp.maximum(best, peak_x[k])
            peak_own[3] = best
            c_line = pltpu.make_async_remote_copy(
                src_ref=peak_own.at[3],
                dst_ref=peak_c,
                send_sem=c_sem.at[0],
                recv_sem=c_sem.at[1],
                device_id=sibling,
                device_id_type=MESH,
            )
            c_line.start()
    prepare(3)
    for group in range(4):
        here = y ^ group
        value = three(dot, (last[0, here], last[1, here]), (data[0], data[1]))
        rows = pl.ds(pl.multiple_of(here * 64, 64), 64)
        for k2 in range(2):
            lanes = pl.ds(k2 * 128, 128)
            real = value[:64, k2 * 128 : (k2 + 1) * 128]
            imag = value[64:, k2 * 128 : (k2 + 1) * 128]
            size = jnp.sqrt(real * real + imag * imag)
            scale = factor[k2, rows, :] / jnp.maximum(size, FLOOR_LEVEL)
            for ri, part in enumerate((real * scale, imag * scale)):
                at = pl.ds(pl.multiple_of(ri * 256 + here * 64, 64), 64)
                high_part, low_part = split(part)
                again[0, at, lanes] = high_part
                again[1, at, lanes] = low_part
    loads[9].wait()
    own_core = core == 0
    swaps = []

    def inverse_group(group):
        here = y ^ group
        rows = pl.ds(pl.multiple_of(here * 64, 64), 64)
        value = three(dot, (last_back[0, here], last_back[1, here]), (again[0], again[1]))
        parts = []
        for k2 in range(2):
            real = value[:64, k2 * 128 : (k2 + 1) * 128]
            imag = value[64:, k2 * 128 : (k2 + 1) * 128]
            turn_r, turn_i = twiddle[k2, 0, rows, :], twiddle[k2, 1, rows, :]
            parts.append(
                jnp.concatenate(
                    [real * turn_r + imag * turn_i, imag * turn_r - real * turn_i], axis=1
                )
            )
        plus, minus = parts[0] + parts[1], parts[0] - parts[1]
        part_out[rows, :] = jnp.where(own_core, minus, plus)
        part_own[rows, :] = jnp.where(own_core, plus, minus)
        swap = pltpu.make_async_remote_copy(
            src_ref=part_out.at[rows],
            dst_ref=part_in.at[rows],
            send_sem=part_sem.at[group],
            recv_sem=part_sem.at[4 + group],
            device_id=sibling,
            device_id_type=MESH,
        )
        swap.start()
        swaps.append(swap)

    def back_group(group):
        swaps[group].wait_recv()
        here = y ^ group
        rows = pl.ds(pl.multiple_of(here * 64, 64), 64)
        joined = split(jnp.concatenate([part_own[rows, :], part_in[rows, :]], axis=1))
        result = three(dot_t, joined, (mixed[0], mixed[1]))
        for digit in range(4):
            at = pl.ds(pl.multiple_of(here * 256 + digit * 64, 64), 64)
            back_out[at, :] = result[:, digit * 128 : (digit + 1) * 128]
        send_group(back_out, back_in, back_sem, group)
        if group == 0:
            keep_own(back_out, back_in)

    for group in range(3):
        inverse_group(group)
    back_group(0)
    inverse_group(3)
    for group in range(1, 4):
        back_group(group)
    c_line.wait_recv()
    gain = 1.0 / jnp.max(jnp.maximum(best, peak_c[...]))

    loads[11].wait()
    for group in range(4):
        got_group(back_out, back_in, back_sem, group)

    def store_turned(row, value):
        turned[pl.ds(row * 128, 128), :] = value

    first_step(lambda row: back_in[pl.ds(row, 128, stride=8), :], first_back, store_turned)

    def last_step(step, carry):
        for inside in range(8):
            index = step * 8 + inside
            at = pl.ds(pl.multiple_of(index * 128, 128), 128)
            even = turned[pl.ds(index, 8, stride=128), :]
            odd = turned[pl.ds(64 + index, 8, stride=128), :]
            real = jnp.where(lane < 64, even, pltpu.roll(odd, 64, 1))
            imag = jnp.where(lane < 64, pltpu.roll(even, 64, 1), odd)
            chirp_re, chirp_im = chirp_at(at)
            step_re = real * chirp_re + imag * chirp_im - wave[0, :, at]
            step_im = imag * chirp_re - real * chirp_im - wave[1, :, at]
            probe_re, probe_im = probe[0, :, at], probe[1, :, at]
            out_ref[0, :, at] = (probe_re * step_re + probe_im * step_im) * gain
            out_ref[1, :, at] = (probe_re * step_im - probe_im * step_re) * gain
        return carry

    lax.fori_loop(0, 8, last_step, 0)

    for shift in shifts:
        shift.wait_send()
    share.wait_send()
    for copy in z_line + y_line + x_line + mixes + swaps:
        copy.wait_send()
    c_line.wait_send()
    all_of(field_out, field_in, field_sem, 1016).wait_send()
    all_of(back_out, back_in, back_sem, 1016).wait_send()

    @pl.when(core == 0)
    def _():
        all_of(shades_out, field_in, shade_sem, 504).wait_send()

    @pl.when(core == 1)
    def _():
        all_of(shades_out, field_in, shade_sem, 512).wait_send()


def body(object_field, probe, intensity, row_offset, col_offset):
    tables = make_tables()
    constants = [jnp.asarray(tables[name]) for name in TABLES]
    vmem, dma = pltpu.VMEM, pltpu.SemaphoreType.DMA
    anywhere = pl.BlockSpec(memory_space=pltpu.HBM)
    scalar = pl.BlockSpec(memory_space=pltpu.SMEM)
    inside = pl.BlockSpec(memory_space=pltpu.VMEM)
    state = vmem((1024, 128), F32)
    scratch = [
        vmem((2, 8, 8192), F32),
        vmem((2, 8, 8192), F32),
        vmem((2, 8, 8192), F32),
        vmem((2, 1, 8192), F32),
        vmem((2, 8, 256), F32),
        vmem((2, 128, 256), BF16),
        vmem((2, 128, 256), BF16),
        vmem((2, 64, 128), F32),
        vmem((512, 512), F32),
        vmem((2, 4, 128, 512), BF16),
        vmem((2, 4, 128, 512), BF16),
        vmem((2, 2, 256, 128), F32),
        state,
        state,
        vmem((2, 8, 8192), F32),
        state,
        state,
        state,
        vmem((2, 512, 512), BF16),
        vmem((256, 256), F32),
        vmem((256, 256), F32),
        vmem((256, 256), F32),
        vmem((2, 512, 256), BF16),
        vmem((2, 512, 256), BF16),
        vmem((2, 256, 128), F32),
        state,
        state,
        vmem((64, 2, 8, 128), F32),
        state,
        state,
        vmem((256, 256), F32),
        vmem((256, 256), F32),
        vmem((256, 256), F32),
        vmem((4, 8, 128), F32),
        vmem((7, 8, 128), F32),
        vmem((3, 8, 128), F32),
        vmem((3, 8, 128), F32),
        vmem((8, 128), F32),
        dma((13,)),
        dma((4,)),
        dma((2,)),
        dma((14,)),
        dma((6,)),
        dma((6,)),
        dma((2,)),
        dma((5,)),
        dma((8,)),
        dma((5,)),
        dma((8,)),
        dma((8,)),
        dma((5,)),
        dma((1,)),
        pltpu.SemaphoreType.REGULAR((4,)),
    ]
    return pl.pallas_call(
        kernel,
        out_shape=pltpu.VMEM(object_field.shape, F32),
        in_specs=[scalar, scalar] + [anywhere] * (3 + len(constants)),
        out_specs=inside,
        scratch_shapes=scratch,
        compiler_params=pltpu.CompilerParams(
            collective_id=0, has_side_effects=True, vmem_limit_bytes=60 << 20
        ),
        cost_estimate=pl.CostEstimate(
            flops=2_000_000_000, bytes_accessed=8_000_000, transcendentals=200_000
        ),
    )(row_offset, col_offset, object_field, probe, intensity, *constants)


def solution(mesh):
    placed = (
        P(None, ("outer", "inner"), None),
        P(None, ("outer", "inner"), None),
        P(("outer", "inner"), None),
        P(),
        P(),
    )
    return jax.shard_map(
        body,
        mesh=mesh,
        in_specs=placed,
        out_specs=P(None, ("outer", "inner"), None),
        check_vma=False,
    )
```

```python
import math

import jax
import jax.numpy as jnp
import numpy as np
from jax import lax
from jax.experimental import pallas as pl
from jax.experimental.pallas import tpu as pltpu
from jax.sharding import PartitionSpec as P

FLOOR_LEVEL = 0.1
ORDER = (2, 3, 1, 0)
MESH = pl.DeviceIdType.MESH
CHIPS = 128
F32 = jnp.float32
BF16 = jnp.bfloat16


def split_table(table):
    table = np.asarray(table, np.float64).astype(np.float32)
    high = table.astype(jnp.bfloat16)
    low = (table - high.astype(np.float32)).astype(jnp.bfloat16)
    return np.stack([high, low])


def turn(numerator, modulus):
    angle = -2.0 * np.pi * (np.asarray(numerator) % modulus) / modulus
    return np.exp(1j * angle)


def expanded(table):
    return np.block([[table.real, table.imag], [-table.imag, table.real]])


def make_tables():
    tables = {}
    col = np.arange(8192, dtype=np.int64) - 4096
    col_phase = np.pi / 8192 * (col * col % 16384)
    tables["col_chirp"] = np.stack([np.cos(col_phase), np.sin(col_phase)]).reshape(2, 1, 8192).astype(np.float32)
    row = np.arange(2048, dtype=np.int64) - 1024
    row_phase = (np.pi / 2048 * (row * row % 4096)).reshape(256, 8).T
    tables["row_chirp"] = np.stack([np.cos(row_phase), np.sin(row_phase)]).astype(np.float32)
    order = np.concatenate([2 * np.arange(64), 2 * np.arange(64) + 1])
    first = turn(np.arange(128)[:, None] * order[None, :], 128)
    tables["first"] = split_table(np.concatenate([first.real, first.imag], axis=1))
    back = np.conj(first).T
    tables["first_back"] = split_table(np.concatenate([back.real, back.imag], axis=1))
    chip_turn = turn(np.arange(64)[:, None] * np.arange(128)[None, :], 8192)
    tables["chip_turn"] = np.stack([chip_turn.real, chip_turn.imag]).astype(np.float32)
    base = []
    for core in range(2):
        blocks = []
        for zh in range(4):
            halves = []
            for half in range(2):
                q = 32 * (core if half == 0 else 1 - core) + np.arange(32)
                klow = np.arange(4)
                m = np.arange(64)
                power = (
                    m[:, None, None] * q[None, None, :] * 8
                    + zh * klow[None, :, None] * 128
                    + core * klow[None, :, None] * 64
                )
                halves.append(expanded(turn(power, 512).reshape(64, 128)))
            blocks.append(np.concatenate(halves, axis=1))
        base.append(np.concatenate(blocks, axis=0))
    tables["base"] = np.stack(base).astype(np.float32)
    index = np.arange(256)
    y, zl, x, l = index // 64, index // 32 % 2, index // 8 % 4, index % 8
    n = 64 * y + 16 * x + 8 * zl + l
    last = turn(n[:, None] * n[None, :], 256)
    for name, sign in (("last", 1.0), ("last_back", -1.0)):
        whole = np.block([[last.real, -sign * last.imag], [sign * last.imag, last.real]])
        blocks = whole.reshape(2, 4, 64, 512).transpose(1, 0, 2, 3).reshape(4, 128, 512)
        tables[name] = split_table(blocks)
    klow = np.arange(128) // 32
    twiddle = np.stack([turn(n[:, None] * (klow[None, :] + 4 * k2), 2048) for k2 in range(2)]) / 4096.0
    tables["twiddle"] = np.stack([twiddle.real, twiddle.imag], axis=1).astype(np.float32)
    return tables


TABLES = (
    "col_chirp",
    "row_chirp",
    "first",
    "first_back",
    "chip_turn",
    "base",
    "last",
    "last_back",
    "twiddle",
)


def split(value):
    high = value.astype(BF16)
    low = (value - high.astype(F32)).astype(BF16)
    return high, low


def dot(left, right):
    return jnp.dot(left, right, preferred_element_type=F32)


def dot_t(left, right):
    return lax.dot_general(left, right, (((1,), (1,)), ((), ())), preferred_element_type=F32)


def three(op, left, right):
    return op(left[0], right[0]) + (op(left[0], right[1]) + op(left[1], right[0]))


def device_of(chip, core):
    z = chip // 4 % 8
    return (z // 2) * 2 + core, (chip // 32) * 8 + (chip % 4) * 2 + z % 2


def far_first(step):
    swapped = step ^ 2
    return swapped ^ (1 - swapped // 2)


def far_first_of_eight(step):
    return jnp.where(step < 4, step + 4, far_first(step % 4))


def flip(chip, offset):
    return chip ^ offset


def tile(ref, index):
    return ref.at[pl.ds(pl.multiple_of(index * 8, 8), 8)]


def kernel(
    row_off,
    col_off,
    obj_hbm,
    probe_hbm,
    int_hbm,
    col_chirp_hbm,
    row_chirp_hbm,
    first_hbm,
    first_back_hbm,
    chip_turn_hbm,
    base_hbm,
    last_hbm,
    last_back_hbm,
    twiddle_hbm,
    out_ref,
    obj,
    probe,
    inten,
    col_chirp,
    row_chirp,
    first,
    first_back,
    chip_turn,
    base,
    last,
    last_back,
    twiddle,
    rolled,
    arrived,
    wave,
    lifted,
    turned,
    field_out,
    field_in,
    mixed,
    mix_out,
    mix_in,
    mix_kept,
    data,
    again,
    factor,
    spread,
    shades_out,
    shades_in,
    back_out,
    back_in,
    part_out,
    part_in,
    part_own,
    peak_own,
    peak_z,
    peak_y,
    peak_x,
    peak_c,
    load_sem,
    shift_sem,
    int_sem,
    z_sem,
    y_sem,
    x_sem,
    c_sem,
    shade_sem,
    pass_sem,
    field_sem,
    mix_sem,
    part_sem,
    back_sem,
    local_sem,
    gates,
):
    outer, inner = lax.axis_index("outer"), lax.axis_index("inner")
    zh, core = outer // 2, outer % 2
    other = 1 - core
    z, y, x = zh * 2 + inner % 2, inner // 8, inner // 2 % 4
    chip = y * 32 + z * 4 + x
    number = outer * 32 + inner
    after, before = (number + 1) % 256, (number + 255) % 256
    sibling = device_of(chip, other)
    next_device = (after // 32, after % 32)
    last_device = (before // 32, before % 32)

    loads = []
    pairs = (
        (obj_hbm.at[0], obj.at[0]),
        (probe_hbm, probe),
        (int_hbm, inten.at[core]),
        (base_hbm.at[core], base),
        (chip_turn_hbm, chip_turn),
        (col_chirp_hbm, col_chirp),
        (row_chirp_hbm, row_chirp),
        (first_hbm, first),
        (last_hbm, last),
        (last_back_hbm, last_back),
        (twiddle_hbm, twiddle),
        (first_back_hbm, first_back),
        (obj_hbm.at[1], obj.at[1]),
    )
    for slot, (source, target) in enumerate(pairs):
        loads.append(pltpu.make_async_copy(source, target, load_sem.at[slot]))
    for slot in (0, 2, 12):
        loads[slot].start()

    barrier = pltpu.get_barrier_semaphore()

    def at_chip(dz, dy, dx):
        to = (y + dy + 4) % 4 * 32 + (z + dz + 8) % 8 * 4 + (x + dx + 4) % 4
        return device_of(to, core)

    around = [at_chip(*by) for by in ((1, 0, 0), (-1, 0, 0), (0, 1, 0), (0, -1, 0), (0, 0, 1), (0, 0, -1))]
    greeted = around + [sibling, next_device, last_device]
    for device in greeted:
        pl.semaphore_signal(barrier, inc=1, device_id=device, device_id_type=MESH)

    def tell(gate, devices):
        for device in devices:
            pl.semaphore_signal(gate, inc=1, device_id=device, device_id_type=MESH)


    rows_by, cols_by = row_off[0], col_off[0]
    tiles_by, lanes_by = cols_by // 128, cols_by % 128
    lane = lax.broadcasted_iota(jnp.int32, (8, 128), 1)
    sub = lax.broadcasted_iota(jnp.int32, (8, 128), 0)
    for part in range(2):
        for row in (7,):
            arrived[pl.ds(part * 512 + row * 64, 64), :] = jnp.zeros((64, 128), F32)
    wide_lane = lax.broadcasted_iota(jnp.int32, (64, 128), 1)
    shifts = []
    for part in range(2):

        def roll_step(step, carry, part=part):
            for inside in range(8):
                at = step * 8 + inside
                piece = obj[part, :, pl.ds(pl.multiple_of(at * 128, 128), 128)]
                moved = pltpu.roll(pltpu.roll(piece, lanes_by, 1), rows_by, 0)
                rolled[pl.ds(part * 512 + at, 8, stride=64), :] = moved
            return carry

        def tile_step(row, carry, part=part):
            at = pl.ds(pl.multiple_of(part * 512 + row * 64, 64), 64)
            moved = pltpu.roll(rolled[at, :], tiles_by, 0)
            rolled[at, :] = jnp.where(wide_lane < lanes_by, pltpu.roll(moved, 1, 0), moved)
            return carry

        loads[12 * part].wait()
        lax.fori_loop(0, 8, roll_step, 0)
        lax.fori_loop(0, 8, tile_step, 0)
        if part == 0:
            pl.semaphore_wait(barrier, 9)
            tell(gates.at[0], around)
        shift = pltpu.make_async_remote_copy(
            src_ref=rolled.at[pl.ds(part * 512, 448)],
            dst_ref=arrived.at[pl.ds(part * 512, 448)],
            send_sem=shift_sem.at[part],
            recv_sem=shift_sem.at[2 + part],
            device_id=next_device,
            device_id_type=MESH,
        )
        shift.start()
        shifts.append(shift)
        if part == 0:
            loads[2].wait()
            share = pltpu.make_async_remote_copy(
                src_ref=inten.at[core],
                dst_ref=inten.at[core],
                send_sem=int_sem.at[0],
                recv_sem=int_sem.at[1],
                device_id=sibling,
                device_id_type=MESH,
            )
            share.start()
    for slot in (1, 3, 4, 5, 6, 7, 8, 9, 10, 11):
        loads[slot].start()
    pl.semaphore_wait(gates.at[0], 6)
    tell(gates.at[1], [at_chip(2, 0, 0), at_chip(-2, 0, 0)])

    pl.semaphore_wait(gates.at[1], 2)
    tell(gates.at[2], [device_of(flip(chip, k << 5), core) for k in range(1, 4)])
    share.wait_recv()
    for c in range(2):

        def spread_step(step, carry, c=c):
            for inside in range(8):
                at = step * 8 + inside
                piece = inten[c, :, pl.ds(pl.multiple_of(at * 128, 128), 128)]
                spread[pl.ds(c * 64 + at, 8, stride=128), :] = piece
            return carry

        lax.fori_loop(0, 8, spread_step, 0)
    pl.semaphore_wait(gates.at[2], 3)
    tell(gates.at[3], [device_of(flip(chip, k), core) for k in range(1, 4)])
    for l in range(4):
        shades_out[pl.ds(l, 128, stride=8), :] = jnp.transpose(spread[pl.ds(l * 128, 128), :])

    for l in range(4, 8):
        shades_out[pl.ds(l, 128, stride=8), :] = jnp.transpose(spread[pl.ds(l * 128, 128), :])
    pl.semaphore_wait(gates.at[3], 3)

    def send_shades(group):
        def shade_step(step, carry):
            offset = far_first_of_eight(step % 8) * 4 + (1 - step // 8) * 2 + core
            target = flip(chip, group * 32 + offset)
            pltpu.make_async_remote_copy(
                src_ref=tile(shades_out, target),
                dst_ref=shades_in.at[chip // 2, chip % 2],
                send_sem=shade_sem.at[0],
                recv_sem=shade_sem.at[1 + group],
                device_id=device_of(target, core),
                device_id_type=MESH,
            ).start()
            return carry

        lax.fori_loop(0, 15 + core if group == 0 else 16, shade_step, 0)

    for group in ORDER:
        send_shades(group)

    @pl.when(core == 0)
    def _():
        own = pltpu.make_async_copy(
            tile(shades_out, chip), shades_in.at[chip // 2, chip % 2], local_sem.at[0]
        )
        own.start()
        own.wait()

    loads[1].wait()

    def peak_step(step, best):
        for inside in range(8):
            at = pl.ds(pl.multiple_of((step * 8 + inside) * 128, 128), 128)
            real, imag = probe[0, :, at], probe[1, :, at]
            best = jnp.maximum(best, real * real + imag * imag)
        return best

    peak_own[0] = lax.fori_loop(0, 8, peak_step, jnp.zeros((8, 128), F32))

    loads[3].wait()
    loads[4].wait()
    chip_lane = lax.broadcasted_iota(jnp.int32, (64, 128), 1) == chip
    turn_re = jnp.sum(jnp.where(chip_lane, chip_turn[0], 0.0), axis=1, keepdims=True)
    turn_im = jnp.sum(jnp.where(chip_lane, chip_turn[1], 0.0), axis=1, keepdims=True)
    for block in range(4):
        low, high = pl.ds(block * 128, 64), pl.ds(block * 128 + 64, 64)
        for_re, for_im = base[low, :], base[high, :]
        for at, value in (
            (low, for_re * turn_re + for_im * turn_im),
            (high, for_im * turn_re - for_re * turn_im),
        ):
            high_part, low_part = split(value)
            mixed[0, at, :] = high_part
            mixed[1, at, :] = low_part

    for slot in (5, 6, 7):
        loads[slot].wait()
    number_lane = lax.broadcasted_iota(jnp.int32, (8, 256), 1) == number
    row_re = jnp.sum(jnp.where(number_lane, row_chirp[0], 0.0), axis=1, keepdims=True)
    row_im = jnp.sum(jnp.where(number_lane, row_chirp[1], 0.0), axis=1, keepdims=True)

    def chirp_at(at):
        col_re, col_im = col_chirp[0, :, at], col_chirp[1, :, at]
        return row_re * col_re - row_im * col_im, row_re * col_im + row_im * col_re

    def lift_step(step, carry):
        for inside in range(8):
            index = step * 8 + inside
            at = pl.ds(pl.multiple_of(index * 128, 128), 128)
            probe_re, probe_im = probe[0, :, at], probe[1, :, at]
            chirp_re, chirp_im = chirp_at(at)
            lifted[pl.ds(index, 8, stride=64), :] = probe_re * chirp_re - probe_im * chirp_im
            lifted[pl.ds(512 + index, 8, stride=64), :] = probe_re * chirp_im + probe_im * chirp_re
        return carry

    lax.fori_loop(0, 8, lift_step, 0)

    for shift in shifts:
        shift.wait_recv()
    left = wide_lane < 64

    def wave_row(row, carry):
        re_at = pl.ds(pl.multiple_of(row * 64, 64), 64)
        im_at = pl.ds(pl.multiple_of(512 + row * 64, 64), 64)
        from_before = jnp.full((64, 128), row, jnp.int32) < rows_by
        view_re = jnp.where(from_before, arrived[re_at, :], rolled[re_at, :])
        view_im = jnp.where(from_before, arrived[im_at, :], rolled[im_at, :])
        lift_re, lift_im = lifted[re_at, :], lifted[im_at, :]
        real = lift_re * view_re - lift_im * view_im
        imag = lift_re * view_im + lift_im * view_re
        even = jnp.where(left, real, pltpu.roll(imag, 64, 1))
        odd = jnp.where(left, pltpu.roll(real, 64, 1), imag)
        turned[pl.ds(pl.multiple_of(row * 128, 128), 64), :] = even
        turned[pl.ds(pl.multiple_of(row * 128 + 64, 64), 64), :] = odd
        return carry

    lax.fori_loop(0, 8, wave_row, 0)

    def times_i(value):
        half = lax.broadcasted_iota(jnp.int32, value.shape, 1) < 64
        moved = pltpu.roll(value, 64, 1)
        return jnp.where(half, -moved, moved)

    def first_step(load, table, store):
        for pair in range(4):
            sides = []
            for row in (2 * pair, 2 * pair + 1):
                value = load(row)
                sides.append(jnp.concatenate([value, times_i(value)], axis=0))
            result = three(dot, (table[0], table[1]), split(jnp.concatenate(sides, axis=1)))
            store(2 * pair, result[:, :128])
            store(2 * pair + 1, result[:, 128:])

    def store_field(row, value):
        field_out[pl.ds(row, 128, stride=8), :] = value

    first_step(lambda row: turned[pl.ds(row * 128, 128), :], first, store_field)

    def send_group(source, target, sem, group):
        def send_step(step, carry):
            offset = group * 32 + far_first_of_eight(step % 8) * 4 + far_first(step // 8)
            to = flip(chip, offset)
            pltpu.make_async_remote_copy(
                src_ref=tile(source, to),
                dst_ref=tile(target, chip),
                send_sem=sem.at[0],
                recv_sem=sem.at[1 + group],
                device_id=device_of(to, core),
                device_id_type=MESH,
            ).start()
            return carry

        lax.fori_loop(0, 31 if group == 0 else 32, send_step, 0)

    def keep_own(source, target):
        own = pltpu.make_async_copy(tile(source, chip), tile(target, chip), local_sem.at[0])
        own.start()
        own.wait()

    def all_of(source, target, sem, rows, group=0):
        return pltpu.make_async_remote_copy(
            src_ref=source.at[pl.ds(0, rows)],
            dst_ref=target.at[pl.ds(0, rows)],
            send_sem=sem.at[0],
            recv_sem=sem.at[1 + group],
            device_id=sibling,
            device_id_type=MESH,
        )

    def got_group(source, target, sem, group):
        all_of(source, target, sem, 248 if group == 0 else 256, group).wait_recv()

    def peak_line(source, target, sem, count, by):
        copies = []
        for k in range(1, count):
            copy = pltpu.make_async_remote_copy(
                src_ref=source,
                dst_ref=target.at[k - 1],
                send_sem=sem.at[k - 1],
                recv_sem=sem.at[count - 2 + k],
                device_id=device_of(flip(chip, k << by), core),
                device_id_type=MESH,
            )
            copy.start()
            copies.append(copy)
        return copies

    z_line = peak_line(peak_own.at[0], peak_z, z_sem, 8, 2)
    for group in ORDER:
        send_group(field_out, field_in, field_sem, group)
    keep_own(field_out, field_in)


    mine = (chip + core) % 2

    def pass_shades(group):
        if group == 0:

            @pl.when(core == 0)
            def _():
                all_of(shades_out, field_in, shade_sem, 120, group).wait_recv()

            @pl.when(core == 1)
            def _():
                all_of(shades_out, field_in, shade_sem, 128, group).wait_recv()

        else:
            all_of(shades_out, field_in, shade_sem, 128, group).wait_recv()
        block = pl.ds((y ^ group) * 16, 16)
        copy = pltpu.make_async_remote_copy(
            src_ref=shades_in.at[block, mine],
            dst_ref=shades_in.at[block, mine],
            send_sem=pass_sem.at[group],
            recv_sem=pass_sem.at[4 + group],
            device_id=sibling,
            device_id_type=MESH,
        )
        copy.start()
        return copy

    lane_group = lax.broadcasted_iota(jnp.int32, (64, 128), 1) // 32

    def make_factor(group):
        for c in range(2):
            shade = jnp.zeros((64, 128), F32)
            for digit in range(4):
                want = 2 * (digit % 2) + digit // 2
                by = (32 * (want - 2 * c - core) + 128) % 128
                part = shades_in[pl.ds((y ^ group) * 16 + digit * 4, 4)].reshape(64, 128)
                shade = jnp.where(lane_group == want, pltpu.roll(part, by, 1), shade)
            factor[c, pl.ds(pl.multiple_of((y ^ group) * 64, 64), 64), :] = jnp.sqrt(shade)

    for copy in z_line:
        copy.wait_recv()
    best = peak_own[0]
    for k in range(7):
        best = jnp.maximum(best, peak_z[k])
    peak_own[1] = best
    y_line = peak_line(peak_own.at[1], peak_y, y_sem, 4, 5)
    passes = [pass_shades(group) for group in range(4)]
    for copy in y_line:
        copy.wait_recv()
    for k in range(3):
        best = jnp.maximum(best, peak_y[k])
    peak_own[2] = best
    x_line = peak_line(peak_own.at[2], peak_x, x_sem, 4, 0)

    def wave_step(step, carry):
        for inside in range(8):
            index = step * 8 + inside
            at = pl.ds(pl.multiple_of(index * 128, 128), 128)
            views = []
            for part in range(2):
                rows = pl.ds(part * 512 + index, 8, stride=64)
                views.append(jnp.where(sub < rows_by, arrived[rows, :], rolled[rows, :]))
            probe_re, probe_im = probe[0, :, at], probe[1, :, at]
            wave[0, :, at] = probe_re * views[0] - probe_im * views[1]
            wave[1, :, at] = probe_re * views[1] + probe_im * views[0]
        return carry

    lax.fori_loop(0, 8, wave_step, 0)

    sent_half = (mixed.at[0, :, pl.ds(256, 256)], mixed.at[1, :, pl.ds(256, 256)])
    kept_half = (mixed.at[0, :, pl.ds(0, 256)], mixed.at[1, :, pl.ds(0, 256)])
    mixes = []
    sign = jnp.where(core == 0, 1.0, -1.0).astype(F32)
    loads[8].wait()
    loads[10].wait()

    def prepare(turn_at):
        mixes[turn_at].wait_recv()
        here = y ^ ORDER[turn_at]
        rows = pl.ds(pl.multiple_of(here * 64, 64), 64)
        kept, got = mix_kept[rows, :], mix_in[rows, :]
        for k2, total in enumerate((kept + got, (kept - got) * sign)):
            real, imag = total[:, :128], total[:, 128:]
            turn_r, turn_i = twiddle[k2, 0, rows, :], twiddle[k2, 1, rows, :]
            lanes = pl.ds(k2 * 128, 128)
            for ri, value in enumerate(
                (real * turn_r - imag * turn_i, real * turn_i + imag * turn_r)
            ):
                at = pl.ds(pl.multiple_of(ri * 256 + here * 64, 64), 64)
                high_part, low_part = split(value)
                data[0, at, lanes] = high_part
                data[1, at, lanes] = low_part

    for turn_at, group in enumerate(ORDER):
        got_group(field_out, field_in, field_sem, group)
        here = y ^ group
        pieces = [field_in[pl.ds(pl.multiple_of(here * 256 + digit * 64, 64), 64), :] for digit in range(4)]
        joined = split(jnp.concatenate(pieces, axis=1))
        rows = pl.ds(pl.multiple_of(here * 64, 64), 64)
        mix_out[rows, :] = three(dot, joined, (sent_half[0][...], sent_half[1][...]))
        mix = pltpu.make_async_remote_copy(
            src_ref=mix_out.at[rows],
            dst_ref=mix_in.at[rows],
            send_sem=mix_sem.at[turn_at],
            recv_sem=mix_sem.at[4 + turn_at],
            device_id=sibling,
            device_id_type=MESH,
        )
        mix.start()
        mixes.append(mix)
        mix_kept[rows, :] = three(dot, joined, (kept_half[0][...], kept_half[1][...]))
        if turn_at > 0:
            prepare(turn_at - 1)
        else:
            for early in range(4):
                passes[early].wait()
                make_factor(early)
        if turn_at == 1:
            for copy in x_line:
                copy.wait_recv()
            for k in range(3):
                best = jnp.maximum(best, peak_x[k])
            peak_own[3] = best
            c_line = pltpu.make_async_remote_copy(
                src_ref=peak_own.at[3],
                dst_ref=peak_c,
                send_sem=c_sem.at[0],
                recv_sem=c_sem.at[1],
                device_id=sibling,
                device_id_type=MESH,
            )
            c_line.start()
    prepare(3)
    for group in range(4):
        here = y ^ group
        value = three(dot, (last[0, here], last[1, here]), (data[0], data[1]))
        rows = pl.ds(pl.multiple_of(here * 64, 64), 64)
        for k2 in range(2):
            lanes = pl.ds(k2 * 128, 128)
            real = value[:64, k2 * 128 : (k2 + 1) * 128]
            imag = value[64:, k2 * 128 : (k2 + 1) * 128]
            size = jnp.sqrt(real * real + imag * imag)
            scale = factor[k2, rows, :] / jnp.maximum(size, FLOOR_LEVEL)
            for ri, part in enumerate((real * scale, imag * scale)):
                at = pl.ds(pl.multiple_of(ri * 256 + here * 64, 64), 64)
                high_part, low_part = split(part)
                again[0, at, lanes] = high_part
                again[1, at, lanes] = low_part
    loads[9].wait()
    own_core = core == 0
    swaps = []

    def inverse_group(group):
        here = y ^ group
        rows = pl.ds(pl.multiple_of(here * 64, 64), 64)
        value = three(dot, (last_back[0, here], last_back[1, here]), (again[0], again[1]))
        parts = []
        for k2 in range(2):
            real = value[:64, k2 * 128 : (k2 + 1) * 128]
            imag = value[64:, k2 * 128 : (k2 + 1) * 128]
            turn_r, turn_i = twiddle[k2, 0, rows, :], twiddle[k2, 1, rows, :]
            parts.append(
                jnp.concatenate(
                    [real * turn_r + imag * turn_i, imag * turn_r - real * turn_i], axis=1
                )
            )
        plus, minus = parts[0] + parts[1], parts[0] - parts[1]
        part_out[rows, :] = jnp.where(own_core, minus, plus)
        part_own[rows, :] = jnp.where(own_core, plus, minus)
        swap = pltpu.make_async_remote_copy(
            src_ref=part_out.at[rows],
            dst_ref=part_in.at[rows],
            send_sem=part_sem.at[group],
            recv_sem=part_sem.at[4 + group],
            device_id=sibling,
            device_id_type=MESH,
        )
        swap.start()
        swaps.append(swap)

    def back_group(group):
        swaps[ORDER.index(group)].wait_recv()
        here = y ^ group
        rows = pl.ds(pl.multiple_of(here * 64, 64), 64)
        joined = split(jnp.concatenate([part_own[rows, :], part_in[rows, :]], axis=1))
        result = three(dot_t, joined, (mixed[0], mixed[1]))
        for digit in range(4):
            at = pl.ds(pl.multiple_of(here * 256 + digit * 64, 64), 64)
            back_out[at, :] = result[:, digit * 128 : (digit + 1) * 128]
        send_group(back_out, back_in, back_sem, group)
        if group == 0:
            keep_own(back_out, back_in)

    for group in ORDER[:3]:
        inverse_group(group)
    back_group(ORDER[0])
    inverse_group(ORDER[3])
    for group in ORDER[1:]:
        back_group(group)
    c_line.wait_recv()
    gain = 1.0 / jnp.max(jnp.maximum(best, peak_c[...]))

    loads[11].wait()
    for group in range(4):
        got_group(back_out, back_in, back_sem, group)

    def store_turned(row, value):
        turned[pl.ds(row * 128, 128), :] = value

    first_step(lambda row: back_in[pl.ds(row, 128, stride=8), :], first_back, store_turned)

    def last_step(step, carry):
        for inside in range(8):
            index = step * 8 + inside
            at = pl.ds(pl.multiple_of(index * 128, 128), 128)
            even = turned[pl.ds(index, 8, stride=128), :]
            odd = turned[pl.ds(64 + index, 8, stride=128), :]
            real = jnp.where(lane < 64, even, pltpu.roll(odd, 64, 1))
            imag = jnp.where(lane < 64, pltpu.roll(even, 64, 1), odd)
            chirp_re, chirp_im = chirp_at(at)
            step_re = real * chirp_re + imag * chirp_im - wave[0, :, at]
            step_im = imag * chirp_re - real * chirp_im - wave[1, :, at]
            probe_re, probe_im = probe[0, :, at], probe[1, :, at]
            out_ref[0, :, at] = (probe_re * step_re + probe_im * step_im) * gain
            out_ref[1, :, at] = (probe_re * step_im - probe_im * step_re) * gain
        return carry

    lax.fori_loop(0, 8, last_step, 0)

    for shift in shifts:
        shift.wait_send()
    share.wait_send()
    for copy in z_line + y_line + x_line + mixes + swaps:
        copy.wait_send()
    c_line.wait_send()
    all_of(field_out, field_in, field_sem, 1016).wait_send()
    all_of(back_out, back_in, back_sem, 1016).wait_send()

    @pl.when(core == 0)
    def _():
        all_of(shades_out, field_in, shade_sem, 504).wait_send()

    @pl.when(core == 1)
    def _():
        all_of(shades_out, field_in, shade_sem, 512).wait_send()


def body(object_field, probe, intensity, row_offset, col_offset):
    tables = make_tables()
    constants = [jnp.asarray(tables[name]) for name in TABLES]
    vmem, dma = pltpu.VMEM, pltpu.SemaphoreType.DMA
    anywhere = pl.BlockSpec(memory_space=pltpu.HBM)
    scalar = pl.BlockSpec(memory_space=pltpu.SMEM)
    inside = pl.BlockSpec(memory_space=pltpu.VMEM)
    state = vmem((1024, 128), F32)
    scratch = [
        vmem((2, 8, 8192), F32),
        vmem((2, 8, 8192), F32),
        vmem((2, 8, 8192), F32),
        vmem((2, 1, 8192), F32),
        vmem((2, 8, 256), F32),
        vmem((2, 128, 256), BF16),
        vmem((2, 128, 256), BF16),
        vmem((2, 64, 128), F32),
        vmem((512, 512), F32),
        vmem((2, 4, 128, 512), BF16),
        vmem((2, 4, 128, 512), BF16),
        vmem((2, 2, 256, 128), F32),
        state,
        state,
        vmem((2, 8, 8192), F32),
        state,
        state,
        state,
        state,
        vmem((2, 512, 512), BF16),
        vmem((256, 256), F32),
        vmem((256, 256), F32),
        vmem((256, 256), F32),
        vmem((2, 512, 256), BF16),
        vmem((2, 512, 256), BF16),
        vmem((2, 256, 128), F32),
        state,
        state,
        vmem((64, 2, 8, 128), F32),
        state,
        state,
        vmem((256, 256), F32),
        vmem((256, 256), F32),
        vmem((256, 256), F32),
        vmem((4, 8, 128), F32),
        vmem((7, 8, 128), F32),
        vmem((3, 8, 128), F32),
        vmem((3, 8, 128), F32),
        vmem((8, 128), F32),
        dma((13,)),
        dma((4,)),
        dma((2,)),
        dma((14,)),
        dma((6,)),
        dma((6,)),
        dma((2,)),
        dma((5,)),
        dma((8,)),
        dma((5,)),
        dma((8,)),
        dma((8,)),
        dma((5,)),
        dma((1,)),
        pltpu.SemaphoreType.REGULAR((4,)),
    ]
    return pl.pallas_call(
        kernel,
        out_shape=pltpu.VMEM(object_field.shape, F32),
        in_specs=[scalar, scalar] + [anywhere] * (3 + len(constants)),
        out_specs=inside,
        scratch_shapes=scratch,
        compiler_params=pltpu.CompilerParams(
            collective_id=0, has_side_effects=True, vmem_limit_bytes=60 << 20
        ),
        cost_estimate=pl.CostEstimate(
            flops=2_000_000_000, bytes_accessed=8_000_000, transcendentals=200_000
        ),
    )(row_offset, col_offset, object_field, probe, intensity, *constants)


def solution(mesh):
    placed = (
        P(None, ("outer", "inner"), None),
        P(None, ("outer", "inner"), None),
        P(("outer", "inner"), None),
        P(),
        P(),
    )
    return jax.shard_map(
        body,
        mesh=mesh,
        in_specs=placed,
        out_specs=P(None, ("outer", "inner"), None),
        check_vma=False,
    )
```

```python
import math

import jax
import jax.numpy as jnp
import numpy as np
from jax import lax
from jax.experimental import pallas as pl
from jax.experimental.pallas import tpu as pltpu
from jax.sharding import PartitionSpec as P

FLOOR_LEVEL = 0.1
ORDER = (2, 3, 1, 0)
MESH = pl.DeviceIdType.MESH
CHIPS = 128
F32 = jnp.float32
BF16 = jnp.bfloat16


def split_table(table):
    table = np.asarray(table, np.float64).astype(np.float32)
    high = table.astype(jnp.bfloat16)
    low = (table - high.astype(np.float32)).astype(jnp.bfloat16)
    return np.stack([high, low])


def turn(numerator, modulus):
    angle = -2.0 * np.pi * (np.asarray(numerator) % modulus) / modulus
    return np.exp(1j * angle)


def expanded(table):
    return np.block([[table.real, table.imag], [-table.imag, table.real]])


def make_tables():
    tables = {}
    col = np.arange(8192, dtype=np.int64) - 4096
    col_phase = np.pi / 8192 * (col * col % 16384)
    tables["col_chirp"] = np.stack([np.cos(col_phase), np.sin(col_phase)]).reshape(2, 1, 8192).astype(np.float32)
    row = np.arange(2048, dtype=np.int64) - 1024
    row_phase = (np.pi / 2048 * (row * row % 4096)).reshape(256, 8).T
    tables["row_chirp"] = np.stack([np.cos(row_phase), np.sin(row_phase)]).astype(np.float32)
    order = np.concatenate([2 * np.arange(64), 2 * np.arange(64) + 1])
    first = turn(np.arange(128)[:, None] * order[None, :], 128)
    tables["first"] = split_table(np.concatenate([first.real, first.imag], axis=1))
    back = np.conj(first).T
    tables["first_back"] = split_table(np.concatenate([back.real, back.imag], axis=1))
    chip_turn = turn(np.arange(64)[:, None] * np.arange(128)[None, :], 8192)
    tables["chip_turn"] = np.stack([chip_turn.real, chip_turn.imag]).astype(np.float32)
    base = []
    for core in range(2):
        blocks = []
        for zh in range(4):
            halves = []
            for half in range(2):
                q = 32 * (core if half == 0 else 1 - core) + np.arange(32)
                klow = np.arange(4)
                m = np.arange(64)
                power = (
                    m[:, None, None] * q[None, None, :] * 8
                    + zh * klow[None, :, None] * 128
                    + core * klow[None, :, None] * 64
                )
                halves.append(expanded(turn(power, 512).reshape(64, 128)))
            blocks.append(np.concatenate(halves, axis=1))
        base.append(np.concatenate(blocks, axis=0))
    tables["base"] = np.stack(base).astype(np.float32)
    index = np.arange(256)
    y, zl, x, l = index // 64, index // 32 % 2, index // 8 % 4, index % 8
    n = 64 * y + 16 * x + 8 * zl + l
    last = turn(n[:, None] * n[None, :], 256)
    for name, sign in (("last", 1.0), ("last_back", -1.0)):
        whole = np.block([[last.real, -sign * last.imag], [sign * last.imag, last.real]])
        blocks = whole.reshape(2, 4, 64, 512).transpose(1, 0, 2, 3).reshape(4, 128, 512)
        tables[name] = split_table(blocks)
    klow = np.arange(128) // 32
    twiddle = np.stack([turn(n[:, None] * (klow[None, :] + 4 * k2), 2048) for k2 in range(2)]) / 4096.0
    tables["twiddle"] = np.stack([twiddle.real, twiddle.imag], axis=1).astype(np.float32)
    return tables


TABLES = (
    "col_chirp",
    "row_chirp",
    "first",
    "first_back",
    "chip_turn",
    "base",
    "last",
    "last_back",
    "twiddle",
)


def split(value):
    high = value.astype(BF16)
    low = (value - high.astype(F32)).astype(BF16)
    return high, low


def dot(left, right):
    return jnp.dot(left, right, preferred_element_type=F32)


def dot_t(left, right):
    return lax.dot_general(left, right, (((1,), (1,)), ((), ())), preferred_element_type=F32)


def three(op, left, right):
    return op(left[0], right[0]) + (op(left[0], right[1]) + op(left[1], right[0]))


def device_of(chip, core):
    z = chip // 4 % 8
    return (z // 2) * 2 + core, (chip // 32) * 8 + (chip % 4) * 2 + z % 2


def far_first(step):
    swapped = step ^ 2
    return swapped ^ (1 - swapped // 2)


def far_first_of_eight(step):
    return jnp.where(step < 4, step + 4, far_first(step % 4))


def flip(chip, offset):
    return chip ^ offset


def tile(ref, index):
    return ref.at[pl.ds(pl.multiple_of(index * 8, 8), 8)]


def kernel(
    row_off,
    col_off,
    obj_hbm,
    probe_hbm,
    int_hbm,
    col_chirp_hbm,
    row_chirp_hbm,
    first_hbm,
    first_back_hbm,
    chip_turn_hbm,
    base_hbm,
    last_hbm,
    last_back_hbm,
    twiddle_hbm,
    out_ref,
    obj,
    probe,
    inten,
    col_chirp,
    row_chirp,
    first,
    first_back,
    chip_turn,
    base,
    last,
    last_back,
    twiddle,
    rolled,
    arrived,
    wave,
    lifted,
    turned,
    field_out,
    field_in,
    mixed,
    mix_out,
    mix_in,
    mix_kept,
    data,
    again,
    factor,
    spread,
    shades_out,
    shades_in,
    back_out,
    back_in,
    part_out,
    part_in,
    part_own,
    landed,
    peak_own,
    peak_z,
    peak_y,
    peak_x,
    peak_c,
    load_sem,
    shift_sem,
    int_sem,
    z_sem,
    y_sem,
    x_sem,
    c_sem,
    shade_sem,
    pass_sem,
    field_sem,
    mix_sem,
    part_sem,
    back_sem,
    local_sem,
    gates,
):
    outer, inner = lax.axis_index("outer"), lax.axis_index("inner")
    zh, core = outer // 2, outer % 2
    other = 1 - core
    z, y, x = zh * 2 + inner % 2, inner // 8, inner // 2 % 4
    chip = y * 32 + z * 4 + x
    number = outer * 32 + inner
    after, before = (number + 1) % 256, (number + 255) % 256
    sibling = device_of(chip, other)
    next_device = (after // 32, after % 32)
    last_device = (before // 32, before % 32)

    loads = []
    pairs = (
        (obj_hbm.at[0], obj.at[0]),
        (probe_hbm, probe),
        (int_hbm, inten.at[core]),
        (base_hbm.at[core], base),
        (chip_turn_hbm, chip_turn),
        (col_chirp_hbm, col_chirp),
        (row_chirp_hbm, row_chirp),
        (first_hbm, first),
        (last_hbm, last),
        (last_back_hbm, last_back),
        (twiddle_hbm, twiddle),
        (first_back_hbm, first_back),
        (obj_hbm.at[1], obj.at[1]),
    )
    for slot, (source, target) in enumerate(pairs):
        loads.append(pltpu.make_async_copy(source, target, load_sem.at[slot]))
    for slot in (0, 2, 12):
        loads[slot].start()

    barrier = pltpu.get_barrier_semaphore()

    def at_chip(dz, dy, dx):
        to = (y + dy + 4) % 4 * 32 + (z + dz + 8) % 8 * 4 + (x + dx + 4) % 4
        return device_of(to, core)

    around = [at_chip(*by) for by in ((1, 0, 0), (-1, 0, 0), (0, 1, 0), (0, -1, 0), (0, 0, 1), (0, 0, -1))]
    greeted = around + [sibling, next_device, last_device]
    for device in greeted:
        pl.semaphore_signal(barrier, inc=1, device_id=device, device_id_type=MESH)

    def tell(gate, devices):
        for device in devices:
            pl.semaphore_signal(gate, inc=1, device_id=device, device_id_type=MESH)


    rows_by, cols_by = row_off[0], col_off[0]
    tiles_by, lanes_by = cols_by // 128, cols_by % 128
    lane = lax.broadcasted_iota(jnp.int32, (8, 128), 1)
    sub = lax.broadcasted_iota(jnp.int32, (8, 128), 0)
    for part in range(2):
        for row in (7,):
            arrived[pl.ds(part * 512 + row * 64, 64), :] = jnp.zeros((64, 128), F32)
    wide_lane = lax.broadcasted_iota(jnp.int32, (64, 128), 1)
    shifts = []
    for part in range(2):

        def roll_step(step, carry, part=part):
            for inside in range(8):
                at = step * 8 + inside
                piece = obj[part, :, pl.ds(pl.multiple_of(at * 128, 128), 128)]
                moved = pltpu.roll(pltpu.roll(piece, lanes_by, 1), rows_by, 0)
                rolled[pl.ds(part * 512 + at, 8, stride=64), :] = moved
            return carry

        def tile_step(row, carry, part=part):
            at = pl.ds(pl.multiple_of(part * 512 + row * 64, 64), 64)
            moved = pltpu.roll(rolled[at, :], tiles_by, 0)
            rolled[at, :] = jnp.where(wide_lane < lanes_by, pltpu.roll(moved, 1, 0), moved)
            return carry

        loads[12 * part].wait()
        lax.fori_loop(0, 8, roll_step, 0)
        lax.fori_loop(0, 8, tile_step, 0)
        if part == 0:
            pl.semaphore_wait(barrier, 9)
            tell(gates.at[0], around)
        shift = pltpu.make_async_remote_copy(
            src_ref=rolled.at[pl.ds(part * 512, 448)],
            dst_ref=arrived.at[pl.ds(part * 512, 448)],
            send_sem=shift_sem.at[part],
            recv_sem=shift_sem.at[2 + part],
            device_id=next_device,
            device_id_type=MESH,
        )
        shift.start()
        shifts.append(shift)
        if part == 0:
            loads[2].wait()
            share = pltpu.make_async_remote_copy(
                src_ref=inten.at[core],
                dst_ref=inten.at[core],
                send_sem=int_sem.at[0],
                recv_sem=int_sem.at[1],
                device_id=sibling,
                device_id_type=MESH,
            )
            share.start()
    for slot in (1, 3, 4, 5, 6, 7, 8, 9, 10, 11):
        loads[slot].start()
    pl.semaphore_wait(gates.at[0], 6)
    tell(gates.at[1], [at_chip(2, 0, 0), at_chip(-2, 0, 0)])

    pl.semaphore_wait(gates.at[1], 2)
    tell(gates.at[2], [device_of(flip(chip, k << 5), core) for k in range(1, 4)])
    share.wait_recv()
    for c in range(2):

        def spread_step(step, carry, c=c):
            for inside in range(8):
                at = step * 8 + inside
                piece = inten[c, :, pl.ds(pl.multiple_of(at * 128, 128), 128)]
                spread[pl.ds(c * 64 + at, 8, stride=128), :] = piece
            return carry

        lax.fori_loop(0, 8, spread_step, 0)
    pl.semaphore_wait(gates.at[2], 3)
    tell(gates.at[3], [device_of(flip(chip, k), core) for k in range(1, 4)])
    for l in range(4):
        shades_out[pl.ds(l, 128, stride=8), :] = jnp.transpose(spread[pl.ds(l * 128, 128), :])

    for l in range(4, 8):
        shades_out[pl.ds(l, 128, stride=8), :] = jnp.transpose(spread[pl.ds(l * 128, 128), :])
    pl.semaphore_wait(gates.at[3], 3)

    def send_shades(group):
        def shade_step(step, carry):
            offset = far_first_of_eight(step % 8) * 4 + (1 - step // 8) * 2 + core
            target = flip(chip, group * 32 + offset)
            pltpu.make_async_remote_copy(
                src_ref=tile(shades_out, target),
                dst_ref=shades_in.at[chip // 2, chip % 2],
                send_sem=shade_sem.at[0],
                recv_sem=shade_sem.at[1 + group],
                device_id=device_of(target, core),
                device_id_type=MESH,
            ).start()
            return carry

        lax.fori_loop(0, 15 + core if group == 0 else 16, shade_step, 0)

    for group in ORDER:
        send_shades(group)

    @pl.when(core == 0)
    def _():
        own = pltpu.make_async_copy(
            tile(shades_out, chip), shades_in.at[chip // 2, chip % 2], local_sem.at[0]
        )
        own.start()
        own.wait()

    loads[1].wait()

    def peak_step(step, best):
        for inside in range(8):
            at = pl.ds(pl.multiple_of((step * 8 + inside) * 128, 128), 128)
            real, imag = probe[0, :, at], probe[1, :, at]
            best = jnp.maximum(best, real * real + imag * imag)
        return best

    peak_own[0] = lax.fori_loop(0, 8, peak_step, jnp.zeros((8, 128), F32))

    loads[3].wait()
    loads[4].wait()
    chip_lane = lax.broadcasted_iota(jnp.int32, (64, 128), 1) == chip
    turn_re = jnp.sum(jnp.where(chip_lane, chip_turn[0], 0.0), axis=1, keepdims=True)
    turn_im = jnp.sum(jnp.where(chip_lane, chip_turn[1], 0.0), axis=1, keepdims=True)
    for block in range(4):
        low, high = pl.ds(block * 128, 64), pl.ds(block * 128 + 64, 64)
        for_re, for_im = base[low, :], base[high, :]
        for at, value in (
            (low, for_re * turn_re + for_im * turn_im),
            (high, for_im * turn_re - for_re * turn_im),
        ):
            high_part, low_part = split(value)
            mixed[0, at, :] = high_part
            mixed[1, at, :] = low_part

    for slot in (5, 6, 7):
        loads[slot].wait()
    number_lane = lax.broadcasted_iota(jnp.int32, (8, 256), 1) == number
    row_re = jnp.sum(jnp.where(number_lane, row_chirp[0], 0.0), axis=1, keepdims=True)
    row_im = jnp.sum(jnp.where(number_lane, row_chirp[1], 0.0), axis=1, keepdims=True)

    def chirp_at(at):
        col_re, col_im = col_chirp[0, :, at], col_chirp[1, :, at]
        return row_re * col_re - row_im * col_im, row_re * col_im + row_im * col_re

    def lift_step(step, carry):
        for inside in range(8):
            index = step * 8 + inside
            at = pl.ds(pl.multiple_of(index * 128, 128), 128)
            probe_re, probe_im = probe[0, :, at], probe[1, :, at]
            chirp_re, chirp_im = chirp_at(at)
            lifted[pl.ds(index, 8, stride=64), :] = probe_re * chirp_re - probe_im * chirp_im
            lifted[pl.ds(512 + index, 8, stride=64), :] = probe_re * chirp_im + probe_im * chirp_re
        return carry

    lax.fori_loop(0, 8, lift_step, 0)

    for shift in shifts:
        shift.wait_recv()
    left = wide_lane < 64

    def wave_row(row, carry):
        re_at = pl.ds(pl.multiple_of(row * 64, 64), 64)
        im_at = pl.ds(pl.multiple_of(512 + row * 64, 64), 64)
        from_before = jnp.full((64, 128), row, jnp.int32) < rows_by
        view_re = jnp.where(from_before, arrived[re_at, :], rolled[re_at, :])
        view_im = jnp.where(from_before, arrived[im_at, :], rolled[im_at, :])
        lift_re, lift_im = lifted[re_at, :], lifted[im_at, :]
        real = lift_re * view_re - lift_im * view_im
        imag = lift_re * view_im + lift_im * view_re
        even = jnp.where(left, real, pltpu.roll(imag, 64, 1))
        odd = jnp.where(left, pltpu.roll(real, 64, 1), imag)
        turned[pl.ds(pl.multiple_of(row * 128, 128), 64), :] = even
        turned[pl.ds(pl.multiple_of(row * 128 + 64, 64), 64), :] = odd
        return carry

    lax.fori_loop(0, 8, wave_row, 0)

    def times_i(value):
        half = lax.broadcasted_iota(jnp.int32, value.shape, 1) < 64
        moved = pltpu.roll(value, 64, 1)
        return jnp.where(half, -moved, moved)

    def first_step(load, table, store):
        for pair in range(4):
            sides = []
            for row in (2 * pair, 2 * pair + 1):
                value = load(row)
                sides.append(jnp.concatenate([value, times_i(value)], axis=0))
            result = three(dot, (table[0], table[1]), split(jnp.concatenate(sides, axis=1)))
            store(2 * pair, result[:, :128])
            store(2 * pair + 1, result[:, 128:])

    def store_field(row, value):
        field_out[pl.ds(row, 128, stride=8), :] = value

    first_step(lambda row: turned[pl.ds(row * 128, 128), :], first, store_field)

    def send_group(source, target, sem, group):
        def send_step(step, carry):
            offset = group * 32 + far_first_of_eight(step % 8) * 4 + far_first(step // 8)
            to = flip(chip, offset)
            pltpu.make_async_remote_copy(
                src_ref=tile(source, to),
                dst_ref=tile(target, chip),
                send_sem=sem.at[0],
                recv_sem=sem.at[1 + group],
                device_id=device_of(to, core),
                device_id_type=MESH,
            ).start()
            return carry

        lax.fori_loop(0, 31 if group == 0 else 32, send_step, 0)

    def keep_own(source, target):
        own = pltpu.make_async_copy(tile(source, chip), tile(target, chip), local_sem.at[0])
        own.start()
        own.wait()

    def all_of(source, target, sem, rows, group=0):
        return pltpu.make_async_remote_copy(
            src_ref=source.at[pl.ds(0, rows)],
            dst_ref=target.at[pl.ds(0, rows)],
            send_sem=sem.at[0],
            recv_sem=sem.at[1 + group],
            device_id=sibling,
            device_id_type=MESH,
        )

    def got_group(source, target, sem, group):
        all_of(source, target, sem, 248 if group == 0 else 256, group).wait_recv()

    def peak_line(source, target, sem, count, by):
        copies = []
        for k in range(1, count):
            copy = pltpu.make_async_remote_copy(
                src_ref=source,
                dst_ref=target.at[k - 1],
                send_sem=sem.at[k - 1],
                recv_sem=sem.at[count - 2 + k],
                device_id=device_of(flip(chip, k << by), core),
                device_id_type=MESH,
            )
            copy.start()
            copies.append(copy)
        return copies

    z_line = peak_line(peak_own.at[0], peak_z, z_sem, 8, 2)
    for group in ORDER:
        send_group(field_out, field_in, field_sem, group)
    keep_own(field_out, field_in)


    mine = (chip + core) % 2

    def pass_shades(group):
        if group == 0:

            @pl.when(core == 0)
            def _():
                all_of(shades_out, field_in, shade_sem, 120, group).wait_recv()

            @pl.when(core == 1)
            def _():
                all_of(shades_out, field_in, shade_sem, 128, group).wait_recv()

        else:
            all_of(shades_out, field_in, shade_sem, 128, group).wait_recv()
        block = pl.ds((y ^ group) * 16, 16)
        copy = pltpu.make_async_remote_copy(
            src_ref=shades_in.at[block, mine],
            dst_ref=shades_in.at[block, mine],
            send_sem=pass_sem.at[group],
            recv_sem=pass_sem.at[4 + group],
            device_id=sibling,
            device_id_type=MESH,
        )
        copy.start()
        return copy

    lane_group = lax.broadcasted_iota(jnp.int32, (64, 128), 1) // 32

    def make_factor(group):
        for c in range(2):
            shade = jnp.zeros((64, 128), F32)
            for digit in range(4):
                want = 2 * (digit % 2) + digit // 2
                by = (32 * (want - 2 * c - core) + 128) % 128
                part = shades_in[pl.ds((y ^ group) * 16 + digit * 4, 4)].reshape(64, 128)
                shade = jnp.where(lane_group == want, pltpu.roll(part, by, 1), shade)
            factor[c, pl.ds(pl.multiple_of((y ^ group) * 64, 64), 64), :] = jnp.sqrt(shade)

    for copy in z_line:
        copy.wait_recv()
    best = peak_own[0]
    for k in range(7):
        best = jnp.maximum(best, peak_z[k])
    peak_own[1] = best
    y_line = peak_line(peak_own.at[1], peak_y, y_sem, 4, 5)
    passes = [pass_shades(group) for group in range(4)]
    for copy in y_line:
        copy.wait_recv()
    for k in range(3):
        best = jnp.maximum(best, peak_y[k])
    peak_own[2] = best
    x_line = peak_line(peak_own.at[2], peak_x, x_sem, 4, 0)

    def wave_step(step, carry):
        for inside in range(8):
            index = step * 8 + inside
            at = pl.ds(pl.multiple_of(index * 128, 128), 128)
            views = []
            for part in range(2):
                rows = pl.ds(part * 512 + index, 8, stride=64)
                views.append(jnp.where(sub < rows_by, arrived[rows, :], rolled[rows, :]))
            probe_re, probe_im = probe[0, :, at], probe[1, :, at]
            wave[0, :, at] = probe_re * views[0] - probe_im * views[1]
            wave[1, :, at] = probe_re * views[1] + probe_im * views[0]
        return carry

    lax.fori_loop(0, 8, wave_step, 0)

    sent_half = (mixed.at[0, :, pl.ds(256, 256)], mixed.at[1, :, pl.ds(256, 256)])
    kept_half = (mixed.at[0, :, pl.ds(0, 256)], mixed.at[1, :, pl.ds(0, 256)])
    mixes = []
    sign = jnp.where(core == 0, 1.0, -1.0).astype(F32)
    loads[8].wait()
    loads[10].wait()

    def prepare(turn_at):
        mixes[turn_at].wait_recv()
        here = y ^ ORDER[turn_at]
        rows = pl.ds(pl.multiple_of(here * 64, 64), 64)
        kept, got = mix_kept[rows, :], mix_in[rows, :]
        for k2, total in enumerate((kept + got, (kept - got) * sign)):
            real, imag = total[:, :128], total[:, 128:]
            turn_r, turn_i = twiddle[k2, 0, rows, :], twiddle[k2, 1, rows, :]
            lanes = pl.ds(k2 * 128, 128)
            for ri, value in enumerate(
                (real * turn_r - imag * turn_i, real * turn_i + imag * turn_r)
            ):
                at = pl.ds(pl.multiple_of(ri * 256 + here * 64, 64), 64)
                high_part, low_part = split(value)
                data[0, at, lanes] = high_part
                data[1, at, lanes] = low_part

    for turn_at, group in enumerate(ORDER):
        got_group(field_out, field_in, field_sem, group)
        here = y ^ group
        pieces = [field_in[pl.ds(pl.multiple_of(here * 256 + digit * 64, 64), 64), :] for digit in range(4)]
        joined = split(jnp.concatenate(pieces, axis=1))
        rows = pl.ds(pl.multiple_of(here * 64, 64), 64)
        mix_out[rows, :] = three(dot, joined, (sent_half[0][...], sent_half[1][...]))
        mix = pltpu.make_async_remote_copy(
            src_ref=mix_out.at[rows],
            dst_ref=mix_in.at[rows],
            send_sem=mix_sem.at[turn_at],
            recv_sem=mix_sem.at[4 + turn_at],
            device_id=sibling,
            device_id_type=MESH,
        )
        mix.start()
        mixes.append(mix)
        mix_kept[rows, :] = three(dot, joined, (kept_half[0][...], kept_half[1][...]))
        if turn_at > 0:
            prepare(turn_at - 1)
        else:
            for early in range(4):
                passes[early].wait()
                make_factor(early)
        if turn_at == 1:
            for copy in x_line:
                copy.wait_recv()
            for k in range(3):
                best = jnp.maximum(best, peak_x[k])
            peak_own[3] = best
            c_line = pltpu.make_async_remote_copy(
                src_ref=peak_own.at[3],
                dst_ref=peak_c,
                send_sem=c_sem.at[0],
                recv_sem=c_sem.at[1],
                device_id=sibling,
                device_id_type=MESH,
            )
            c_line.start()
    prepare(3)
    for group in range(4):
        here = y ^ group
        value = three(dot, (last[0, here], last[1, here]), (data[0], data[1]))
        rows = pl.ds(pl.multiple_of(here * 64, 64), 64)
        for k2 in range(2):
            lanes = pl.ds(k2 * 128, 128)
            real = value[:64, k2 * 128 : (k2 + 1) * 128]
            imag = value[64:, k2 * 128 : (k2 + 1) * 128]
            size = jnp.sqrt(real * real + imag * imag)
            scale = factor[k2, rows, :] / jnp.maximum(size, FLOOR_LEVEL)
            for ri, part in enumerate((real * scale, imag * scale)):
                at = pl.ds(pl.multiple_of(ri * 256 + here * 64, 64), 64)
                high_part, low_part = split(part)
                again[0, at, lanes] = high_part
                again[1, at, lanes] = low_part
    loads[9].wait()
    own_core = core == 0
    swaps = []

    def inverse_group(group):
        here = y ^ group
        rows = pl.ds(pl.multiple_of(here * 64, 64), 64)
        value = three(dot, (last_back[0, here], last_back[1, here]), (again[0], again[1]))
        parts = []
        for k2 in range(2):
            real = value[:64, k2 * 128 : (k2 + 1) * 128]
            imag = value[64:, k2 * 128 : (k2 + 1) * 128]
            turn_r, turn_i = twiddle[k2, 0, rows, :], twiddle[k2, 1, rows, :]
            parts.append(
                jnp.concatenate(
                    [real * turn_r + imag * turn_i, imag * turn_r - real * turn_i], axis=1
                )
            )
        plus, minus = parts[0] + parts[1], parts[0] - parts[1]
        part_out[rows, :] = jnp.where(own_core, minus, plus)
        part_own[rows, :] = jnp.where(own_core, plus, minus)
        swap = pltpu.make_async_remote_copy(
            src_ref=part_out.at[rows],
            dst_ref=part_in.at[rows],
            send_sem=part_sem.at[group],
            recv_sem=part_sem.at[4 + group],
            device_id=sibling,
            device_id_type=MESH,
        )
        swap.start()
        swaps.append(swap)

    def back_group(group):
        swaps[ORDER.index(group)].wait_recv()
        here = y ^ group
        rows = pl.ds(pl.multiple_of(here * 64, 64), 64)
        joined = split(jnp.concatenate([part_own[rows, :], part_in[rows, :]], axis=1))
        result = three(dot_t, joined, (mixed[0], mixed[1]))
        for digit in range(4):
            at = pl.ds(pl.multiple_of(here * 256 + digit * 64, 64), 64)
            back_out[at, :] = result[:, digit * 128 : (digit + 1) * 128]
        send_group(back_out, back_in, back_sem, group)
        if group == 0:
            keep_own(back_out, back_in)

    for group in ORDER[:3]:
        inverse_group(group)
    back_group(ORDER[0])
    inverse_group(ORDER[3])
    for group in ORDER[1:]:
        back_group(group)
    c_line.wait_recv()
    gain = 1.0 / jnp.max(jnp.maximum(best, peak_c[...]))

    loads[11].wait()
    for group in ORDER:
        got_group(back_out, back_in, back_sem, group)
        here = y ^ group
        for row in range(8):
            value = back_in[pl.ds(here * 256 + row, 32, stride=8), :]
            lanes = pl.ds(row % 2 * 128, 128)
            for base_at, part in ((0, value), (128, times_i(value))):
                at = pl.ds(pl.multiple_of(base_at + here * 32, 32), 32)
                high_part, low_part = split(part)
                landed[0, row // 2, at, lanes] = high_part
                landed[1, row // 2, at, lanes] = low_part
    for pair in range(4):
        result = three(dot, (first_back[0], first_back[1]), (landed[0, pair], landed[1, pair]))
        turned[pl.ds(2 * pair * 128, 128), :] = result[:, :128]
        turned[pl.ds((2 * pair + 1) * 128, 128), :] = result[:, 128:]

    def last_step(step, carry):
        for inside in range(8):
            index = step * 8 + inside
            at = pl.ds(pl.multiple_of(index * 128, 128), 128)
            even = turned[pl.ds(index, 8, stride=128), :]
            odd = turned[pl.ds(64 + index, 8, stride=128), :]
            real = jnp.where(lane < 64, even, pltpu.roll(odd, 64, 1))
            imag = jnp.where(lane < 64, pltpu.roll(even, 64, 1), odd)
            chirp_re, chirp_im = chirp_at(at)
            step_re = real * chirp_re + imag * chirp_im - wave[0, :, at]
            step_im = imag * chirp_re - real * chirp_im - wave[1, :, at]
            probe_re, probe_im = probe[0, :, at], probe[1, :, at]
            out_ref[0, :, at] = (probe_re * step_re + probe_im * step_im) * gain
            out_ref[1, :, at] = (probe_re * step_im - probe_im * step_re) * gain
        return carry

    lax.fori_loop(0, 8, last_step, 0)

    for shift in shifts:
        shift.wait_send()
    share.wait_send()
    for copy in z_line + y_line + x_line + mixes + swaps:
        copy.wait_send()
    c_line.wait_send()
    all_of(field_out, field_in, field_sem, 1016).wait_send()
    all_of(back_out, back_in, back_sem, 1016).wait_send()

    @pl.when(core == 0)
    def _():
        all_of(shades_out, field_in, shade_sem, 504).wait_send()

    @pl.when(core == 1)
    def _():
        all_of(shades_out, field_in, shade_sem, 512).wait_send()


def body(object_field, probe, intensity, row_offset, col_offset):
    tables = make_tables()
    constants = [jnp.asarray(tables[name]) for name in TABLES]
    vmem, dma = pltpu.VMEM, pltpu.SemaphoreType.DMA
    anywhere = pl.BlockSpec(memory_space=pltpu.HBM)
    scalar = pl.BlockSpec(memory_space=pltpu.SMEM)
    inside = pl.BlockSpec(memory_space=pltpu.VMEM)
    state = vmem((1024, 128), F32)
    scratch = [
        vmem((2, 8, 8192), F32),
        vmem((2, 8, 8192), F32),
        vmem((2, 8, 8192), F32),
        vmem((2, 1, 8192), F32),
        vmem((2, 8, 256), F32),
        vmem((2, 128, 256), BF16),
        vmem((2, 128, 256), BF16),
        vmem((2, 64, 128), F32),
        vmem((512, 512), F32),
        vmem((2, 4, 128, 512), BF16),
        vmem((2, 4, 128, 512), BF16),
        vmem((2, 2, 256, 128), F32),
        state,
        state,
        vmem((2, 8, 8192), F32),
        state,
        state,
        state,
        state,
        vmem((2, 512, 512), BF16),
        vmem((256, 256), F32),
        vmem((256, 256), F32),
        vmem((256, 256), F32),
        vmem((2, 512, 256), BF16),
        vmem((2, 512, 256), BF16),
        vmem((2, 256, 128), F32),
        state,
        state,
        vmem((64, 2, 8, 128), F32),
        state,
        state,
        vmem((256, 256), F32),
        vmem((256, 256), F32),
        vmem((256, 256), F32),
        vmem((2, 4, 256, 256), BF16),
        vmem((4, 8, 128), F32),
        vmem((7, 8, 128), F32),
        vmem((3, 8, 128), F32),
        vmem((3, 8, 128), F32),
        vmem((8, 128), F32),
        dma((13,)),
        dma((4,)),
        dma((2,)),
        dma((14,)),
        dma((6,)),
        dma((6,)),
        dma((2,)),
        dma((5,)),
        dma((8,)),
        dma((5,)),
        dma((8,)),
        dma((8,)),
        dma((5,)),
        dma((1,)),
        pltpu.SemaphoreType.REGULAR((4,)),
    ]
    return pl.pallas_call(
        kernel,
        out_shape=pltpu.VMEM(object_field.shape, F32),
        in_specs=[scalar, scalar] + [anywhere] * (3 + len(constants)),
        out_specs=inside,
        scratch_shapes=scratch,
        compiler_params=pltpu.CompilerParams(
            collective_id=0, has_side_effects=True, vmem_limit_bytes=60 << 20
        ),
        cost_estimate=pl.CostEstimate(
            flops=2_000_000_000, bytes_accessed=8_000_000, transcendentals=200_000
        ),
    )(row_offset, col_offset, object_field, probe, intensity, *constants)


def solution(mesh):
    placed = (
        P(None, ("outer", "inner"), None),
        P(None, ("outer", "inner"), None),
        P(("outer", "inner"), None),
        P(),
        P(),
    )
    return jax.shard_map(
        body,
        mesh=mesh,
        in_specs=placed,
        out_specs=P(None, ("outer", "inner"), None),
        check_vma=False,
    )
```

```python
import math

import jax
import jax.numpy as jnp
import numpy as np
from jax import lax
from jax.experimental import pallas as pl
from jax.experimental.pallas import tpu as pltpu
from jax.sharding import PartitionSpec as P

FLOOR_LEVEL = 0.1
ORDER = (2, 3, 1, 0)
MESH = pl.DeviceIdType.MESH
CHIPS = 128
F32 = jnp.float32
BF16 = jnp.bfloat16


def split_table(table):
    table = np.asarray(table, np.float64).astype(np.float32)
    high = table.astype(jnp.bfloat16)
    low = (table - high.astype(np.float32)).astype(jnp.bfloat16)
    return np.stack([high, low])


def turn(numerator, modulus):
    angle = -2.0 * np.pi * (np.asarray(numerator) % modulus) / modulus
    return np.exp(1j * angle)


def expanded(table):
    return np.block([[table.real, table.imag], [-table.imag, table.real]])


def make_tables():
    tables = {}
    col = np.arange(8192, dtype=np.int64) - 4096
    col_phase = np.pi / 8192 * (col * col % 16384)
    tables["col_chirp"] = np.stack([np.cos(col_phase), np.sin(col_phase)]).reshape(2, 1, 8192).astype(np.float32)
    row = np.arange(2048, dtype=np.int64) - 1024
    row_phase = (np.pi / 2048 * (row * row % 4096)).reshape(256, 8).T
    tables["row_chirp"] = np.stack([np.cos(row_phase), np.sin(row_phase)]).astype(np.float32)
    order = np.concatenate([2 * np.arange(64), 2 * np.arange(64) + 1])
    first = turn(np.arange(128)[:, None] * order[None, :], 128)
    tables["first"] = split_table(np.concatenate([first.real, first.imag], axis=1))
    back = np.conj(first).T
    tables["first_back"] = split_table(np.concatenate([back.real, back.imag], axis=1))
    chip_turn = turn(np.arange(64)[:, None] * np.arange(128)[None, :], 8192)
    tables["chip_turn"] = np.stack([chip_turn.real, chip_turn.imag]).astype(np.float32)
    base = []
    for core in range(2):
        blocks = []
        for zh in range(4):
            halves = []
            for half in range(2):
                q = 32 * (core if half == 0 else 1 - core) + np.arange(32)
                klow = np.arange(4)
                m = np.arange(64)
                power = (
                    m[:, None, None] * q[None, None, :] * 8
                    + zh * klow[None, :, None] * 128
                    + core * klow[None, :, None] * 64
                )
                halves.append(expanded(turn(power, 512).reshape(64, 128)))
            blocks.append(np.concatenate(halves, axis=1))
        base.append(np.concatenate(blocks, axis=0))
    tables["base"] = np.stack(base).astype(np.float32)
    index = np.arange(256)
    y, zl, x, l = index // 64, index // 32 % 2, index // 8 % 4, index % 8
    n = 64 * y + 16 * x + 8 * zl + l
    last = turn(n[:, None] * n[None, :], 256)
    for name, sign in (("last", 1.0), ("last_back", -1.0)):
        whole = np.block([[last.real, -sign * last.imag], [sign * last.imag, last.real]])
        blocks = whole.reshape(2, 4, 64, 512).transpose(1, 0, 2, 3).reshape(4, 128, 512)
        if name == "last":
            blocks = blocks.reshape(4, 128, 2, 4, 64).transpose(0, 3, 1, 2, 4).reshape(4, 4, 128, 128)
        tables[name] = split_table(blocks)
    klow = np.arange(128) // 32
    twiddle = np.stack([turn(n[:, None] * (klow[None, :] + 4 * k2), 2048) for k2 in range(2)]) / 4096.0
    tables["twiddle"] = np.stack([twiddle.real, twiddle.imag], axis=1).astype(np.float32)
    return tables


TABLES = (
    "col_chirp",
    "row_chirp",
    "first",
    "first_back",
    "chip_turn",
    "base",
    "last",
    "last_back",
    "twiddle",
)


def split(value):
    high = value.astype(BF16)
    low = (value - high.astype(F32)).astype(BF16)
    return high, low


def dot(left, right):
    return jnp.dot(left, right, preferred_element_type=F32)


def dot_t(left, right):
    return lax.dot_general(left, right, (((1,), (1,)), ((), ())), preferred_element_type=F32)


def three(op, left, right):
    return op(left[0], right[0]) + (op(left[0], right[1]) + op(left[1], right[0]))


def device_of(chip, core):
    z = chip // 4 % 8
    return (z // 2) * 2 + core, (chip // 32) * 8 + (chip % 4) * 2 + z % 2


def far_first(step):
    swapped = step ^ 2
    return swapped ^ (1 - swapped // 2)


def far_first_of_eight(step):
    return jnp.where(step < 4, step + 4, far_first(step % 4))


def flip(chip, offset):
    return chip ^ offset


def tile(ref, index):
    return ref.at[pl.ds(pl.multiple_of(index * 8, 8), 8)]


def kernel(
    row_off,
    col_off,
    obj_hbm,
    probe_hbm,
    int_hbm,
    col_chirp_hbm,
    row_chirp_hbm,
    first_hbm,
    first_back_hbm,
    chip_turn_hbm,
    base_hbm,
    last_hbm,
    last_back_hbm,
    twiddle_hbm,
    out_ref,
    obj,
    probe,
    inten,
    col_chirp,
    row_chirp,
    first,
    first_back,
    chip_turn,
    base,
    last,
    last_back,
    twiddle,
    rolled,
    arrived,
    wave,
    lifted,
    turned,
    field_out,
    field_in,
    mixed,
    mix_out,
    mix_in,
    mix_kept,
    data,
    partial,
    again,
    factor,
    spread,
    shades_out,
    shades_in,
    back_out,
    back_in,
    part_out,
    part_in,
    part_own,
    landed,
    peak_own,
    peak_z,
    peak_y,
    peak_x,
    peak_c,
    load_sem,
    shift_sem,
    int_sem,
    z_sem,
    y_sem,
    x_sem,
    c_sem,
    shade_sem,
    pass_sem,
    field_sem,
    mix_sem,
    part_sem,
    back_sem,
    local_sem,
    gates,
):
    outer, inner = lax.axis_index("outer"), lax.axis_index("inner")
    zh, core = outer // 2, outer % 2
    other = 1 - core
    z, y, x = zh * 2 + inner % 2, inner // 8, inner // 2 % 4
    chip = y * 32 + z * 4 + x
    number = outer * 32 + inner
    after, before = (number + 1) % 256, (number + 255) % 256
    sibling = device_of(chip, other)
    next_device = (after // 32, after % 32)
    last_device = (before // 32, before % 32)

    loads = []
    pairs = (
        (obj_hbm.at[0], obj.at[0]),
        (probe_hbm, probe),
        (int_hbm, inten.at[core]),
        (base_hbm.at[core], base),
        (chip_turn_hbm, chip_turn),
        (col_chirp_hbm, col_chirp),
        (row_chirp_hbm, row_chirp),
        (first_hbm, first),
        (last_hbm, last),
        (last_back_hbm, last_back),
        (twiddle_hbm, twiddle),
        (first_back_hbm, first_back),
        (obj_hbm.at[1], obj.at[1]),
    )
    for slot, (source, target) in enumerate(pairs):
        loads.append(pltpu.make_async_copy(source, target, load_sem.at[slot]))
    for slot in (0, 2, 12):
        loads[slot].start()

    barrier = pltpu.get_barrier_semaphore()

    def at_chip(dz, dy, dx):
        to = (y + dy + 4) % 4 * 32 + (z + dz + 8) % 8 * 4 + (x + dx + 4) % 4
        return device_of(to, core)

    around = [at_chip(*by) for by in ((1, 0, 0), (-1, 0, 0), (0, 1, 0), (0, -1, 0), (0, 0, 1), (0, 0, -1))]
    greeted = around + [sibling, next_device, last_device]
    for device in greeted:
        pl.semaphore_signal(barrier, inc=1, device_id=device, device_id_type=MESH)

    def tell(gate, devices):
        for device in devices:
            pl.semaphore_signal(gate, inc=1, device_id=device, device_id_type=MESH)


    rows_by, cols_by = row_off[0], col_off[0]
    tiles_by, lanes_by = cols_by // 128, cols_by % 128
    lane = lax.broadcasted_iota(jnp.int32, (8, 128), 1)
    sub = lax.broadcasted_iota(jnp.int32, (8, 128), 0)
    for part in range(2):
        for row in (7,):
            arrived[pl.ds(part * 512 + row * 64, 64), :] = jnp.zeros((64, 128), F32)
    wide_lane = lax.broadcasted_iota(jnp.int32, (64, 128), 1)
    shifts = []
    for part in range(2):

        def roll_step(step, carry, part=part):
            for inside in range(8):
                at = step * 8 + inside
                piece = obj[part, :, pl.ds(pl.multiple_of(at * 128, 128), 128)]
                moved = pltpu.roll(pltpu.roll(piece, lanes_by, 1), rows_by, 0)
                rolled[pl.ds(part * 512 + at, 8, stride=64), :] = moved
            return carry

        def tile_step(row, carry, part=part):
            at = pl.ds(pl.multiple_of(part * 512 + row * 64, 64), 64)
            moved = pltpu.roll(rolled[at, :], tiles_by, 0)
            rolled[at, :] = jnp.where(wide_lane < lanes_by, pltpu.roll(moved, 1, 0), moved)
            return carry

        loads[12 * part].wait()
        lax.fori_loop(0, 8, roll_step, 0)
        lax.fori_loop(0, 8, tile_step, 0)
        if part == 0:
            pl.semaphore_wait(barrier, 9)
            tell(gates.at[0], around)
        shift = pltpu.make_async_remote_copy(
            src_ref=rolled.at[pl.ds(part * 512, 448)],
            dst_ref=arrived.at[pl.ds(part * 512, 448)],
            send_sem=shift_sem.at[part],
            recv_sem=shift_sem.at[2 + part],
            device_id=next_device,
            device_id_type=MESH,
        )
        shift.start()
        shifts.append(shift)
        if part == 0:
            loads[2].wait()
            share = pltpu.make_async_remote_copy(
                src_ref=inten.at[core],
                dst_ref=inten.at[core],
                send_sem=int_sem.at[0],
                recv_sem=int_sem.at[1],
                device_id=sibling,
                device_id_type=MESH,
            )
            share.start()
    for slot in (1, 3, 4, 5, 6, 7, 8, 9, 10, 11):
        loads[slot].start()
    pl.semaphore_wait(gates.at[0], 6)
    tell(gates.at[1], [at_chip(2, 0, 0), at_chip(-2, 0, 0)])

    pl.semaphore_wait(gates.at[1], 2)
    tell(gates.at[2], [device_of(flip(chip, k << 5), core) for k in range(1, 4)])
    share.wait_recv()
    for c in range(2):

        def spread_step(step, carry, c=c):
            for inside in range(8):
                at = step * 8 + inside
                piece = inten[c, :, pl.ds(pl.multiple_of(at * 128, 128), 128)]
                spread[pl.ds(c * 64 + at, 8, stride=128), :] = piece
            return carry

        lax.fori_loop(0, 8, spread_step, 0)
    pl.semaphore_wait(gates.at[2], 3)
    tell(gates.at[3], [device_of(flip(chip, k), core) for k in range(1, 4)])
    for l in range(4):
        shades_out[pl.ds(l, 128, stride=8), :] = jnp.transpose(spread[pl.ds(l * 128, 128), :])

    for l in range(4, 8):
        shades_out[pl.ds(l, 128, stride=8), :] = jnp.transpose(spread[pl.ds(l * 128, 128), :])
    pl.semaphore_wait(gates.at[3], 3)

    def send_shades(group):
        def shade_step(step, carry):
            offset = far_first_of_eight(step % 8) * 4 + (1 - step // 8) * 2 + core
            target = flip(chip, group * 32 + offset)
            pltpu.make_async_remote_copy(
                src_ref=tile(shades_out, target),
                dst_ref=shades_in.at[chip // 2, chip % 2],
                send_sem=shade_sem.at[0],
                recv_sem=shade_sem.at[1 + group],
                device_id=device_of(target, core),
                device_id_type=MESH,
            ).start()
            return carry

        lax.fori_loop(0, 15 + core if group == 0 else 16, shade_step, 0)

    for group in ORDER:
        send_shades(group)

    @pl.when(core == 0)
    def _():
        own = pltpu.make_async_copy(
            tile(shades_out, chip), shades_in.at[chip // 2, chip % 2], local_sem.at[0]
        )
        own.start()
        own.wait()

    loads[1].wait()

    def peak_step(step, best):
        for inside in range(8):
            at = pl.ds(pl.multiple_of((step * 8 + inside) * 128, 128), 128)
            real, imag = probe[0, :, at], probe[1, :, at]
            best = jnp.maximum(best, real * real + imag * imag)
        return best

    peak_own[0] = lax.fori_loop(0, 8, peak_step, jnp.zeros((8, 128), F32))

    loads[3].wait()
    loads[4].wait()
    chip_lane = lax.broadcasted_iota(jnp.int32, (64, 128), 1) == chip
    turn_re = jnp.sum(jnp.where(chip_lane, chip_turn[0], 0.0), axis=1, keepdims=True)
    turn_im = jnp.sum(jnp.where(chip_lane, chip_turn[1], 0.0), axis=1, keepdims=True)
    for block in range(4):
        low, high = pl.ds(block * 128, 64), pl.ds(block * 128 + 64, 64)
        for_re, for_im = base[low, :], base[high, :]
        for at, value in (
            (low, for_re * turn_re + for_im * turn_im),
            (high, for_im * turn_re - for_re * turn_im),
        ):
            high_part, low_part = split(value)
            mixed[0, at, :] = high_part
            mixed[1, at, :] = low_part

    for slot in (5, 6, 7):
        loads[slot].wait()
    number_lane = lax.broadcasted_iota(jnp.int32, (8, 256), 1) == number
    row_re = jnp.sum(jnp.where(number_lane, row_chirp[0], 0.0), axis=1, keepdims=True)
    row_im = jnp.sum(jnp.where(number_lane, row_chirp[1], 0.0), axis=1, keepdims=True)

    def chirp_at(at):
        col_re, col_im = col_chirp[0, :, at], col_chirp[1, :, at]
        return row_re * col_re - row_im * col_im, row_re * col_im + row_im * col_re

    def lift_step(step, carry):
        for inside in range(8):
            index = step * 8 + inside
            at = pl.ds(pl.multiple_of(index * 128, 128), 128)
            probe_re, probe_im = probe[0, :, at], probe[1, :, at]
            chirp_re, chirp_im = chirp_at(at)
            lifted[pl.ds(index, 8, stride=64), :] = probe_re * chirp_re - probe_im * chirp_im
            lifted[pl.ds(512 + index, 8, stride=64), :] = probe_re * chirp_im + probe_im * chirp_re
        return carry

    lax.fori_loop(0, 8, lift_step, 0)

    for shift in shifts:
        shift.wait_recv()
    left = wide_lane < 64

    def wave_row(row, carry):
        re_at = pl.ds(pl.multiple_of(row * 64, 64), 64)
        im_at = pl.ds(pl.multiple_of(512 + row * 64, 64), 64)
        from_before = jnp.full((64, 128), row, jnp.int32) < rows_by
        view_re = jnp.where(from_before, arrived[re_at, :], rolled[re_at, :])
        view_im = jnp.where(from_before, arrived[im_at, :], rolled[im_at, :])
        lift_re, lift_im = lifted[re_at, :], lifted[im_at, :]
        real = lift_re * view_re - lift_im * view_im
        imag = lift_re * view_im + lift_im * view_re
        even = jnp.where(left, real, pltpu.roll(imag, 64, 1))
        odd = jnp.where(left, pltpu.roll(real, 64, 1), imag)
        turned[pl.ds(pl.multiple_of(row * 128, 128), 64), :] = even
        turned[pl.ds(pl.multiple_of(row * 128 + 64, 64), 64), :] = odd
        return carry

    lax.fori_loop(0, 8, wave_row, 0)

    def times_i(value):
        half = lax.broadcasted_iota(jnp.int32, value.shape, 1) < 64
        moved = pltpu.roll(value, 64, 1)
        return jnp.where(half, -moved, moved)

    def first_step(load, table, store):
        for pair in range(4):
            sides = []
            for row in (2 * pair, 2 * pair + 1):
                value = load(row)
                sides.append(jnp.concatenate([value, times_i(value)], axis=0))
            result = three(dot, (table[0], table[1]), split(jnp.concatenate(sides, axis=1)))
            store(2 * pair, result[:, :128])
            store(2 * pair + 1, result[:, 128:])

    def store_field(row, value):
        field_out[pl.ds(row, 128, stride=8), :] = value

    first_step(lambda row: turned[pl.ds(row * 128, 128), :], first, store_field)

    def send_group(source, target, sem, group):
        def send_step(step, carry):
            offset = group * 32 + far_first_of_eight(step % 8) * 4 + far_first(step // 8)
            to = flip(chip, offset)
            pltpu.make_async_remote_copy(
                src_ref=tile(source, to),
                dst_ref=tile(target, chip),
                send_sem=sem.at[0],
                recv_sem=sem.at[1 + group],
                device_id=device_of(to, core),
                device_id_type=MESH,
            ).start()
            return carry

        lax.fori_loop(0, 31 if group == 0 else 32, send_step, 0)

    def keep_own(source, target):
        own = pltpu.make_async_copy(tile(source, chip), tile(target, chip), local_sem.at[0])
        own.start()
        own.wait()

    def all_of(source, target, sem, rows, group=0):
        return pltpu.make_async_remote_copy(
            src_ref=source.at[pl.ds(0, rows)],
            dst_ref=target.at[pl.ds(0, rows)],
            send_sem=sem.at[0],
            recv_sem=sem.at[1 + group],
            device_id=sibling,
            device_id_type=MESH,
        )

    def got_group(source, target, sem, group):
        all_of(source, target, sem, 248 if group == 0 else 256, group).wait_recv()

    def peak_line(source, target, sem, count, by):
        copies = []
        for k in range(1, count):
            copy = pltpu.make_async_remote_copy(
                src_ref=source,
                dst_ref=target.at[k - 1],
                send_sem=sem.at[k - 1],
                recv_sem=sem.at[count - 2 + k],
                device_id=device_of(flip(chip, k << by), core),
                device_id_type=MESH,
            )
            copy.start()
            copies.append(copy)
        return copies

    z_line = peak_line(peak_own.at[0], peak_z, z_sem, 8, 2)
    for group in ORDER:
        send_group(field_out, field_in, field_sem, group)
    keep_own(field_out, field_in)


    mine = (chip + core) % 2

    def pass_shades(group):
        if group == 0:

            @pl.when(core == 0)
            def _():
                all_of(shades_out, field_in, shade_sem, 120, group).wait_recv()

            @pl.when(core == 1)
            def _():
                all_of(shades_out, field_in, shade_sem, 128, group).wait_recv()

        else:
            all_of(shades_out, field_in, shade_sem, 128, group).wait_recv()
        block = pl.ds((y ^ group) * 16, 16)
        copy = pltpu.make_async_remote_copy(
            src_ref=shades_in.at[block, mine],
            dst_ref=shades_in.at[block, mine],
            send_sem=pass_sem.at[group],
            recv_sem=pass_sem.at[4 + group],
            device_id=sibling,
            device_id_type=MESH,
        )
        copy.start()
        return copy

    lane_group = lax.broadcasted_iota(jnp.int32, (64, 128), 1) // 32

    def make_factor(group):
        for c in range(2):
            shade = jnp.zeros((64, 128), F32)
            for digit in range(4):
                want = 2 * (digit % 2) + digit // 2
                by = (32 * (want - 2 * c - core) + 128) % 128
                part = shades_in[pl.ds((y ^ group) * 16 + digit * 4, 4)].reshape(64, 128)
                shade = jnp.where(lane_group == want, pltpu.roll(part, by, 1), shade)
            factor[c, pl.ds(pl.multiple_of((y ^ group) * 64, 64), 64), :] = jnp.sqrt(shade)

    for copy in z_line:
        copy.wait_recv()
    best = peak_own[0]
    for k in range(7):
        best = jnp.maximum(best, peak_z[k])
    peak_own[1] = best
    y_line = peak_line(peak_own.at[1], peak_y, y_sem, 4, 5)
    passes = [pass_shades(group) for group in range(4)]
    for copy in y_line:
        copy.wait_recv()
    for k in range(3):
        best = jnp.maximum(best, peak_y[k])
    peak_own[2] = best
    x_line = peak_line(peak_own.at[2], peak_x, x_sem, 4, 0)

    def wave_step(step, carry):
        for inside in range(8):
            index = step * 8 + inside
            at = pl.ds(pl.multiple_of(index * 128, 128), 128)
            views = []
            for part in range(2):
                rows = pl.ds(part * 512 + index, 8, stride=64)
                views.append(jnp.where(sub < rows_by, arrived[rows, :], rolled[rows, :]))
            probe_re, probe_im = probe[0, :, at], probe[1, :, at]
            wave[0, :, at] = probe_re * views[0] - probe_im * views[1]
            wave[1, :, at] = probe_re * views[1] + probe_im * views[0]
        return carry

    lax.fori_loop(0, 8, wave_step, 0)

    sent_half = (mixed.at[0, :, pl.ds(256, 256)], mixed.at[1, :, pl.ds(256, 256)])
    kept_half = (mixed.at[0, :, pl.ds(0, 256)], mixed.at[1, :, pl.ds(0, 256)])
    mixes = []
    sign = jnp.where(core == 0, 1.0, -1.0).astype(F32)
    loads[8].wait()
    loads[10].wait()

    def prepare(turn_at):
        mixes[turn_at].wait_recv()
        here = y ^ ORDER[turn_at]
        rows = pl.ds(pl.multiple_of(here * 64, 64), 64)
        kept, got = mix_kept[rows, :], mix_in[rows, :]
        for k2, total in enumerate((kept + got, (kept - got) * sign)):
            real, imag = total[:, :128], total[:, 128:]
            turn_r, turn_i = twiddle[k2, 0, rows, :], twiddle[k2, 1, rows, :]
            lanes = pl.ds(k2 * 128, 128)
            for ri, value in enumerate(
                (real * turn_r - imag * turn_i, real * turn_i + imag * turn_r)
            ):
                at = pl.ds(ri * 64, 64)
                high_part, low_part = split(value)
                data[0, here, at, lanes] = high_part
                data[1, here, at, lanes] = low_part

    for turn_at, group in enumerate(ORDER):
        got_group(field_out, field_in, field_sem, group)
        here = y ^ group
        pieces = [field_in[pl.ds(pl.multiple_of(here * 256 + digit * 64, 64), 64), :] for digit in range(4)]
        joined = split(jnp.concatenate(pieces, axis=1))
        rows = pl.ds(pl.multiple_of(here * 64, 64), 64)
        mix_out[rows, :] = three(dot, joined, (sent_half[0][...], sent_half[1][...]))
        mix = pltpu.make_async_remote_copy(
            src_ref=mix_out.at[rows],
            dst_ref=mix_in.at[rows],
            send_sem=mix_sem.at[turn_at],
            recv_sem=mix_sem.at[4 + turn_at],
            device_id=sibling,
            device_id_type=MESH,
        )
        mix.start()
        mixes.append(mix)
        mix_kept[rows, :] = three(dot, joined, (kept_half[0][...], kept_half[1][...]))
        if turn_at > 0:
            prepare(turn_at - 1)
        else:
            for early in range(4):
                passes[early].wait()
                make_factor(early)
        if turn_at == 1:
            for copy in x_line:
                copy.wait_recv()
            for k in range(3):
                best = jnp.maximum(best, peak_x[k])
            peak_own[3] = best
            c_line = pltpu.make_async_remote_copy(
                src_ref=peak_own.at[3],
                dst_ref=peak_c,
                send_sem=c_sem.at[0],
                recv_sem=c_sem.at[1],
                device_id=sibling,
                device_id_type=MESH,
            )
            c_line.start()
    ready = [y ^ group for group in ORDER[:3]]
    final = y ^ ORDER[3]
    given = [jnp.concatenate([data[at, q] for q in ready], axis=0) for at in range(2)]
    for here in range(4):
        table = [jnp.concatenate([last[at, here, q] for q in ready], axis=1) for at in range(2)]
        partial[here] = three(dot, table, given)
    prepare(3)
    for group in range(4):
        here = y ^ group
        value = partial[here] + three(
            dot, (last[0, here, final], last[1, here, final]), (data[0, final], data[1, final])
        )
        rows = pl.ds(pl.multiple_of(here * 64, 64), 64)
        for k2 in range(2):
            lanes = pl.ds(k2 * 128, 128)
            real = value[:64, k2 * 128 : (k2 + 1) * 128]
            imag = value[64:, k2 * 128 : (k2 + 1) * 128]
            size = jnp.sqrt(real * real + imag * imag)
            scale = factor[k2, rows, :] / jnp.maximum(size, FLOOR_LEVEL)
            for ri, part in enumerate((real * scale, imag * scale)):
                at = pl.ds(pl.multiple_of(ri * 256 + here * 64, 64), 64)
                high_part, low_part = split(part)
                again[0, at, lanes] = high_part
                again[1, at, lanes] = low_part
    loads[9].wait()
    own_core = core == 0
    swaps = []

    def inverse_group(group):
        here = y ^ group
        rows = pl.ds(pl.multiple_of(here * 64, 64), 64)
        value = three(dot, (last_back[0, here], last_back[1, here]), (again[0], again[1]))
        parts = []
        for k2 in range(2):
            real = value[:64, k2 * 128 : (k2 + 1) * 128]
            imag = value[64:, k2 * 128 : (k2 + 1) * 128]
            turn_r, turn_i = twiddle[k2, 0, rows, :], twiddle[k2, 1, rows, :]
            parts.append(
                jnp.concatenate(
                    [real * turn_r + imag * turn_i, imag * turn_r - real * turn_i], axis=1
                )
            )
        plus, minus = parts[0] + parts[1], parts[0] - parts[1]
        part_out[rows, :] = jnp.where(own_core, minus, plus)
        part_own[rows, :] = jnp.where(own_core, plus, minus)
        swap = pltpu.make_async_remote_copy(
            src_ref=part_out.at[rows],
            dst_ref=part_in.at[rows],
            send_sem=part_sem.at[group],
            recv_sem=part_sem.at[4 + group],
            device_id=sibling,
            device_id_type=MESH,
        )
        swap.start()
        swaps.append(swap)

    def back_group(group):
        swaps[ORDER.index(group)].wait_recv()
        here = y ^ group
        rows = pl.ds(pl.multiple_of(here * 64, 64), 64)
        joined = split(jnp.concatenate([part_own[rows, :], part_in[rows, :]], axis=1))
        result = three(dot_t, joined, (mixed[0], mixed[1]))
        for digit in range(4):
            at = pl.ds(pl.multiple_of(here * 256 + digit * 64, 64), 64)
            back_out[at, :] = result[:, digit * 128 : (digit + 1) * 128]
        send_group(back_out, back_in, back_sem, group)
        if group == 0:
            keep_own(back_out, back_in)

    for group in ORDER[:3]:
        inverse_group(group)
    back_group(ORDER[0])
    inverse_group(ORDER[3])
    for group in ORDER[1:]:
        back_group(group)
    c_line.wait_recv()
    gain = 1.0 / jnp.max(jnp.maximum(best, peak_c[...]))

    loads[11].wait()
    for group in ORDER:
        got_group(back_out, back_in, back_sem, group)
        here = y ^ group
        for row in range(8):
            value = back_in[pl.ds(here * 256 + row, 32, stride=8), :]
            lanes = pl.ds(row % 2 * 128, 128)
            for base_at, part in ((0, value), (128, times_i(value))):
                at = pl.ds(pl.multiple_of(base_at + here * 32, 32), 32)
                high_part, low_part = split(part)
                landed[0, row // 2, at, lanes] = high_part
                landed[1, row // 2, at, lanes] = low_part
    for pair in range(4):
        result = three(dot, (first_back[0], first_back[1]), (landed[0, pair], landed[1, pair]))
        turned[pl.ds(2 * pair * 128, 128), :] = result[:, :128]
        turned[pl.ds((2 * pair + 1) * 128, 128), :] = result[:, 128:]

    def last_step(step, carry):
        for inside in range(8):
            index = step * 8 + inside
            at = pl.ds(pl.multiple_of(index * 128, 128), 128)
            even = turned[pl.ds(index, 8, stride=128), :]
            odd = turned[pl.ds(64 + index, 8, stride=128), :]
            real = jnp.where(lane < 64, even, pltpu.roll(odd, 64, 1))
            imag = jnp.where(lane < 64, pltpu.roll(even, 64, 1), odd)
            chirp_re, chirp_im = chirp_at(at)
            step_re = real * chirp_re + imag * chirp_im - wave[0, :, at]
            step_im = imag * chirp_re - real * chirp_im - wave[1, :, at]
            probe_re, probe_im = probe[0, :, at], probe[1, :, at]
            out_ref[0, :, at] = (probe_re * step_re + probe_im * step_im) * gain
            out_ref[1, :, at] = (probe_re * step_im - probe_im * step_re) * gain
        return carry

    lax.fori_loop(0, 8, last_step, 0)

    for shift in shifts:
        shift.wait_send()
    share.wait_send()
    for copy in z_line + y_line + x_line + mixes + swaps:
        copy.wait_send()
    c_line.wait_send()
    all_of(field_out, field_in, field_sem, 1016).wait_send()
    all_of(back_out, back_in, back_sem, 1016).wait_send()

    @pl.when(core == 0)
    def _():
        all_of(shades_out, field_in, shade_sem, 504).wait_send()

    @pl.when(core == 1)
    def _():
        all_of(shades_out, field_in, shade_sem, 512).wait_send()


def body(object_field, probe, intensity, row_offset, col_offset):
    tables = make_tables()
    constants = [jnp.asarray(tables[name]) for name in TABLES]
    vmem, dma = pltpu.VMEM, pltpu.SemaphoreType.DMA
    anywhere = pl.BlockSpec(memory_space=pltpu.HBM)
    scalar = pl.BlockSpec(memory_space=pltpu.SMEM)
    inside = pl.BlockSpec(memory_space=pltpu.VMEM)
    state = vmem((1024, 128), F32)
    scratch = [
        vmem((2, 8, 8192), F32),
        vmem((2, 8, 8192), F32),
        vmem((2, 8, 8192), F32),
        vmem((2, 1, 8192), F32),
        vmem((2, 8, 256), F32),
        vmem((2, 128, 256), BF16),
        vmem((2, 128, 256), BF16),
        vmem((2, 64, 128), F32),
        vmem((512, 512), F32),
        vmem((2, 4, 4, 128, 128), BF16),
        vmem((2, 4, 128, 512), BF16),
        vmem((2, 2, 256, 128), F32),
        state,
        state,
        vmem((2, 8, 8192), F32),
        state,
        state,
        state,
        state,
        vmem((2, 512, 512), BF16),
        vmem((256, 256), F32),
        vmem((256, 256), F32),
        vmem((256, 256), F32),
        vmem((2, 4, 128, 256), BF16),
        vmem((4, 128, 256), F32),
        vmem((2, 512, 256), BF16),
        vmem((2, 256, 128), F32),
        state,
        state,
        vmem((64, 2, 8, 128), F32),
        state,
        state,
        vmem((256, 256), F32),
        vmem((256, 256), F32),
        vmem((256, 256), F32),
        vmem((2, 4, 256, 256), BF16),
        vmem((4, 8, 128), F32),
        vmem((7, 8, 128), F32),
        vmem((3, 8, 128), F32),
        vmem((3, 8, 128), F32),
        vmem((8, 128), F32),
        dma((13,)),
        dma((4,)),
        dma((2,)),
        dma((14,)),
        dma((6,)),
        dma((6,)),
        dma((2,)),
        dma((5,)),
        dma((8,)),
        dma((5,)),
        dma((8,)),
        dma((8,)),
        dma((5,)),
        dma((1,)),
        pltpu.SemaphoreType.REGULAR((4,)),
    ]
    return pl.pallas_call(
        kernel,
        out_shape=pltpu.VMEM(object_field.shape, F32),
        in_specs=[scalar, scalar] + [anywhere] * (3 + len(constants)),
        out_specs=inside,
        scratch_shapes=scratch,
        compiler_params=pltpu.CompilerParams(
            collective_id=0, has_side_effects=True, vmem_limit_bytes=60 << 20
        ),
        cost_estimate=pl.CostEstimate(
            flops=2_000_000_000, bytes_accessed=8_000_000, transcendentals=200_000
        ),
    )(row_offset, col_offset, object_field, probe, intensity, *constants)


def solution(mesh):
    placed = (
        P(None, ("outer", "inner"), None),
        P(None, ("outer", "inner"), None),
        P(("outer", "inner"), None),
        P(),
        P(),
    )
    return jax.shard_map(
        body,
        mesh=mesh,
        in_specs=placed,
        out_specs=P(None, ("outer", "inner"), None),
        check_vma=False,
    )
```
